32 devices in a mesh: groups: 2 (over x), expert: 16 (over z, y, core).
Axes of the slice: x: 2, y: 2, z: 4, core: 2. Of those that a mesh axis runs over, the one named last changes fastest.
Arguments:
- tokens: bfloat16 [4096, 4096], P(('groups', 'expert')), parts along dimension 0, may hold values from -6 to 6
- token_grad_in: bfloat16 [4096, 4096], P(('groups', 'expert')), parts along dimension 0, may hold values from -6 to 6
- expert_ids: int32 [4096, 1], P(('groups', 'expert')), parts along dimension 0, may hold values from 0 to 4; in each aligned block of 128 rows (0 to 127, 128 to 255, ...) at most 27 rows name the same one
- gate_weight: bfloat16 [16, 4096, 1376], P('expert'), may hold values from -0.09375 to 0.09375
- up_weight: bfloat16 [16, 4096, 1376], P('expert'), may hold values from -0.09375 to 0.09375
- down_weight: bfloat16 [16, 1376, 4096], P('expert'), may hold values from -0.078125 to 0.078125
Outputs:
- input_grad: bfloat16 [4096, 4096], P(('groups', 'expert')), parts along dimension 0
- down_grad: bfloat16 [32, 1376, 4096], P(('groups', 'expert')), parts along dimension 0
The draws below stay inside these ranges and needn't reach their ends.
There are 2 independent parts, one for each index of `groups`. The reference program is written for one: setup_inputs(seed, part) draws one part's arguments, and reference() takes and returns one part's arrays. A program takes and returns all parts, laid end to end along the dimension named above; an argument that names none is the same for every part. Nothing has to cross between parts.
Inputs may be any that keep to these rules, and one draw needn't show every extreme that they name: `expert_ids`: among the 128 tokens of one device no value appears more than 27 times, and some value appears exactly 27 times; 4 marks a token that no routed expert takes.
All inputs are finite; a program needn't handle non-finite values.
Results may differ from the reference program's by a relative error of at most 0.0058.
Values may be sent and summed in bfloat16 or wider, within the bound.
No kernel may reach another device: no remote copies, remote signals or barrier semaphores. Data moves between devices by JAX's collectives and lax.ppermute only.
A program may use at most 128 MiB of HBM per device.

```python
import math
import jax
import jax.numpy as jnp
import numpy as np
from jax import lax

D = 4096
FWIN = 5504
EXPERTS = 4
TOK_DEV = 128
SPLIT = 4
HDEV = 1376
CAP = 27
TOKENS = 2048
N_EXPERT = 16


def block_scale(rng, shape, cuts, least, largest):
    gain, own = 1.0, jax.random.fold_in(rng, 6)
    for position, parts in cuts:
        heights = jnp.exp(jax.random.uniform(jax.random.fold_in(own, position), (parts,), jnp.float32, least / len(cuts), largest / len(cuts)))
        gain = gain * jnp.repeat(heights, shape[position] // parts).reshape([-1 if axis == position else 1 for axis in range(len(shape))])
    return gain


def assign_block(key, own, number, rows, count, top, limit, slope):
    order = jax.random.permutation(key, count)
    packed, common = load_shares(count, rows * top, limit, slope, True), load_shares(count, rows * top, limit, slope, False)
    places = jnp.arange(count)

    def named(tallies, offset_by):
        used = int((tallies > 0).sum())
        fixed = max(1, used // 4)
        shifted = fixed + (places - fixed + offset_by * (used - fixed)) % max(1, count - fixed)
        return jnp.zeros((count,), jnp.int32).at[order[jnp.where(places < fixed, places, shifted)]].set(jnp.asarray(tallies, jnp.int32))

    tallies = jnp.where(number % 4 == 0, named(packed, number // 4), named(common, number - number // 4 - 1))
    mixed = jax.random.permutation(jax.random.fold_in(own, 3), count)
    donor, receiver = mixed[0:count // 2 * 2:2], mixed[1:count // 2 * 2:2]
    room = jnp.minimum(tallies[donor] - 1, limit - tallies[receiver]) // 2
    room = jnp.where((donor == order[0]) | (receiver == order[0]) | (tallies[receiver] == 0), 0, jnp.maximum(room, 0))
    shifted = jax.random.randint(jax.random.fold_in(own, 4), (count // 2,), 0, 1 << 20) % (room + 1)
    tallies = tallies.at[donor].add(-shifted).at[receiver].add(shifted)
    labels = jnp.searchsorted(jnp.cumsum(tallies), jnp.arange(rows * top), side="right").astype(jnp.int32)
    table = labels.reshape(top, rows).T
    table = table[jax.random.permutation(jax.random.fold_in(own, 1), rows)]
    offset_by = jax.random.randint(jax.random.fold_in(own, 2), (rows, 1), 0, top)
    return jnp.take_along_axis(table, (jnp.arange(top)[None, :] + offset_by) % top, axis=1)


def load_shares(number_of, total, most, skew, full):
    loads = [(1 << 20) // math.isqrt(standing ** skew) + 1 for standing in range(1, number_of + 1)]
    largest = most if full else min(most, max(-(-total // number_of), total * loads[0] // sum(loads)))
    least = 1 if total - largest >= number_of - 1 else 0
    given, surplus = [largest] + [least] * (number_of - 1), total - largest - least * (number_of - 1)
    while surplus > 0:
        movable = [i for i in range(1, number_of) if given[i] < largest] or [i for i in range(1, number_of) if given[i] < most]
        whole, remaining = sum([loads[i] for i in movable]), surplus
        for i in movable:
            addition = min(most - given[i], max(1, remaining * loads[i] // whole), surplus)
            given[i] = given[i] + addition
            surplus = surplus - addition
    return np.array(given)


def scatter_about(stream_key, shape, scale, reach, split=(), held_as=jnp.bfloat16):
    drawn = scale * jax.random.normal(stream_key, shape, jnp.float32)
    if split:
        drawn = drawn * block_scale(stream_key, shape, split, -0.22, 0.18)
    return jnp.clip(drawn, -reach, reach).astype(held_as)


def setup_inputs(seed: int = 0, part: int = 0) -> dict:
    keys = jax.random.split(jax.random.key(seed), 7)
    own_keys = jax.random.split(jax.random.fold_in(keys[6], part), 7)
    tokens = scatter_about(own_keys[0], (TOKENS, D), 1.0, 6.0, ((0, 16),))
    token_grad_in = scatter_about(own_keys[1], (TOKENS, D), 1.0, 6.0, ((0, 16),))
    expert_ids_keys = jax.random.split(jax.random.fold_in(own_keys[2], 1), TOKENS // TOK_DEV)
    expert_ids_turns = jax.random.permutation(jax.random.fold_in(own_keys[2], 3), TOKENS // TOK_DEV)
    expert_ids = jax.vmap(lambda own, number: assign_block(jax.random.fold_in(own_keys[2], 2), own, number, TOK_DEV, EXPERTS + 1, 1, CAP, 2))(expert_ids_keys, expert_ids_turns).reshape((TOKENS, 1))
    gate_weight = scatter_about(keys[3], (N_EXPERT, D, HDEV), D ** -0.5, 0.09375, ((0, 16),))
    up_weight = scatter_about(keys[4], (N_EXPERT, D, HDEV), D ** -0.5, 0.09375, ((0, 16),))
    down_weight = scatter_about(keys[5], (N_EXPERT, HDEV, D), FWIN ** -0.5, 0.078125, ((0, 16),))
    return dict(tokens=tokens, token_grad_in=token_grad_in, expert_ids=expert_ids, gate_weight=gate_weight, up_weight=up_weight, down_weight=down_weight)


def expert_pass(pieces):
    rows_x, rows_grad, w_gate, w_up, w_down = pieces
    xf = rows_x.astype(jnp.float32)
    gf = rows_grad.astype(jnp.float32)
    gate_f = w_gate.astype(jnp.float32)
    up_f = w_up.astype(jnp.float32)
    down_f = w_down.astype(jnp.float32)
    gate_pre = jnp.einsum('rd,sdh->srh', xf, gate_f)
    up_value = jnp.einsum('rd,sdh->srh', xf, up_f)
    sigmoid_g = jax.nn.sigmoid(gate_pre)
    activated = gate_pre * sigmoid_g
    hidden = (activated * up_value).astype(jnp.bfloat16)
    hidden_grad = jnp.einsum('rd,shd->srh', gf, down_f)
    up_grad = (hidden_grad * activated).astype(jnp.bfloat16).astype(jnp.float32)
    gate_grad = (hidden_grad * up_value * sigmoid_g * (1.0 + gate_pre * (1.0 - sigmoid_g))).astype(jnp.bfloat16).astype(jnp.float32)
    partial_value = jnp.einsum('srh,sdh->srd', gate_grad, gate_f) + jnp.einsum('srh,sdh->srd', up_grad, up_f)
    partial_value = lax.optimization_barrier(partial_value.astype(jnp.bfloat16))
    summed = jnp.sum(partial_value.astype(jnp.float32), axis=0)
    weight_grad = jnp.einsum('srh,rd->shd', hidden.astype(jnp.float32), gf).astype(jnp.bfloat16)
    return summed, weight_grad


def reference(tokens, token_grad_in, expert_ids, gate_weight, up_weight, down_weight):
    token_ids = expert_ids[:, 0]
    onehot = (token_ids[:, None] == jnp.arange(EXPERTS + 1, dtype=jnp.int32)[None, :]).astype(jnp.int32)
    blocks = onehot.reshape(N_EXPERT, TOK_DEV, EXPERTS + 1)
    before = (jnp.cumsum(blocks, axis=1) - blocks).reshape(TOKENS, EXPERTS + 1)
    slot_index = jnp.sum(before * onehot, axis=1).astype(jnp.int32)
    source = (jnp.arange(TOKENS, dtype=jnp.int32) // TOK_DEV).astype(jnp.int32)
    slot_row = (source * CAP + slot_index).astype(jnp.int32)
    buf_x = jnp.zeros((EXPERTS, N_EXPERT * CAP, D), jnp.bfloat16).at[token_ids, slot_row].set(tokens, mode="drop")
    buf_grad = jnp.zeros((EXPERTS, N_EXPERT * CAP, D), jnp.bfloat16).at[token_ids, slot_row].set(token_grad_in, mode="drop")
    w_gate = gate_weight.reshape(EXPERTS, SPLIT, D, HDEV)
    w_up = up_weight.reshape(EXPERTS, SPLIT, D, HDEV)
    w_down = down_weight.reshape(EXPERTS, SPLIT, HDEV, D)
    summed, weight_grad = lax.map(expert_pass, (buf_x, buf_grad, w_gate, w_up, w_down))
    safe_ids = jnp.minimum(token_ids, EXPERTS - 1).astype(jnp.int32)
    picked = summed[safe_ids, slot_row]
    routed = (token_ids < EXPERTS)[:, None]
    input_grad = jnp.where(routed, picked, jnp.float32(0.0)).astype(jnp.bfloat16)
    down_grad = weight_grad.reshape(N_EXPERT, HDEV, D)
    return input_grad, down_grad
```

```python
import functools

import jax
import jax.numpy as jnp
from jax import lax
from jax.experimental import pallas as pl
from jax.experimental.pallas import tpu as pltpu
from jax.sharding import PartitionSpec as P

EXPERTS = 4
F32, BF16 = jnp.float32, jnp.bfloat16
NT = (((1,), (1,)), ((), ()))
TN = (((0,), (0,)), ((), ()))
VMEM = 56 * 1024 * 1024


def params():
    return pltpu.CompilerParams(vmem_limit_bytes=VMEM, dimension_semantics=("arbitrary",))


def cost(flops, nbytes):
    return pl.CostEstimate(flops=flops, bytes_accessed=nbytes, transcendentals=0)


def whole(shape):
    return pl.BlockSpec(shape, lambda k, s: (0,) * len(shape))


def slot_map(ids, plane, slots, which, capacity):
    rows = ids.shape[0]
    lane = lax.broadcasted_iota(jnp.int32, (rows, 128), 1)
    onehot = jnp.where(ids == lane, 1.0, 0.0)
    row_i = lax.broadcasted_iota(jnp.int32, (rows, rows), 0)
    col_i = lax.broadcasted_iota(jnp.int32, (rows, rows), 1)
    earlier = jnp.where(col_i < row_i, 1.0, 0.0).astype(BF16)
    before = jnp.dot(earlier, onehot.astype(BF16), preferred_element_type=F32)
    slot = jnp.sum(before * onehot, axis=1, keepdims=True).astype(jnp.int32)
    shift = ids - plane
    shift = jnp.where(shift < 0, shift + EXPERTS, shift)
    target = shift * slots + which * capacity + slot
    target = jnp.where(ids < EXPERTS, target, -1)
    place = lax.broadcasted_iota(jnp.int32, (rows, EXPERTS * slots), 1)
    return jnp.where(target == place, 1.0, 0.0).astype(BF16)


def pack(info, ids, other_ids, mine, other, slots, capacity):
    width = mine.shape[1]

    def body(s, ids_ref, oids_ref, mine_ref, other_ref, *outs):
        p = slot_map(ids_ref[...], s[0], slots, s[1], capacity)
        q = slot_map(oids_ref[...], s[0], slots, 1 - s[1], capacity)
        got = lax.dot_general(p, mine_ref[...], TN, preferred_element_type=F32)
        got = got + lax.dot_general(q, other_ref[...], TN, preferred_element_type=F32)
        got = got.astype(BF16)
        for d in range(EXPERTS):
            outs[d][...] = got[d * slots : (d + 1) * slots]

    return pl.pallas_call(
        body,
        grid_spec=pltpu.PrefetchScalarGridSpec(
            num_scalar_prefetch=1,
            grid=(1,),
            in_specs=[whole(a.shape) for a in (ids, other_ids, mine, other)],
            out_specs=[whole((slots, width))] * EXPERTS,
        ),
        out_shape=[jax.ShapeDtypeStruct((slots, width), BF16)] * EXPERTS,
        compiler_params=params(),
        cost_estimate=cost(4 * 256 * 224 * width, 4 * 256 * width),
        name="pack",
    )(info, ids, other_ids, mine, other)


def unpack(info, ids, other_ids, pieces, slots, capacity):
    rows, width = ids.shape[0], pieces[0].shape[1]

    def body(s, ids_ref, oids_ref, *refs):
        p = slot_map(ids_ref[...], s[0], slots, s[1], capacity)
        q = slot_map(oids_ref[...], s[0], slots, 1 - s[1], capacity)
        z = jnp.concatenate([r[...].astype(F32) for r in refs[:EXPERTS]], axis=0).astype(BF16)
        refs[EXPERTS][...] = jnp.dot(p, z, preferred_element_type=F32).astype(BF16)
        refs[EXPERTS + 1][...] = jnp.dot(q, z, preferred_element_type=F32).astype(BF16)

    return pl.pallas_call(
        body,
        grid_spec=pltpu.PrefetchScalarGridSpec(
            num_scalar_prefetch=1,
            grid=(1,),
            in_specs=[whole(a.shape) for a in (ids, other_ids, *pieces)],
            out_specs=[whole((rows, width))] * 2,
        ),
        out_shape=[jax.ShapeDtypeStruct((rows, width), BF16)] * 2,
        compiler_params=params(),
        cost_estimate=cost(4 * 256 * 224 * width, 4 * 256 * width),
        name="unpack",
    )(info, ids, other_ids, *pieces)


def gate_up(info, own, other, w_gate, w_up, hb=512):
    hidden, model = w_gate.shape
    half = model // 2
    sizes = [a.shape[0] for a in own]
    m, n = sum(sizes), len(own)

    def body(s, *refs):
        xo, xt = refs[:n], refs[n : 2 * n]
        g_ref, u_ref, act_ref, dact_ref, hid_ref, xa, xb = refs[2 * n :]

        @pl.when(pl.program_id(0) == 0)
        def _():
            at = 0
            for i, rows in enumerate(sizes):
                xa[at : at + rows] = xo[i][...]
                xb[at : at + rows] = xt[i][...]
                at += rows

        mine = pl.ds(pl.multiple_of(s[1] * half, 128), half)
        others = pl.ds(pl.multiple_of((1 - s[1]) * half, 128), half)
        a, b = xa[...], xb[...]

        def product(w_ref):
            return lax.dot_general(
                a, w_ref[:, mine], NT, preferred_element_type=F32
            ) + lax.dot_general(b, w_ref[:, others], NT, preferred_element_type=F32)

        g, u = product(g_ref), product(u_ref)
        sig = jax.nn.sigmoid(g)
        act = g * sig
        act_ref[...] = act
        dact_ref[...] = u * sig * (1.0 + g * (1.0 - sig))
        hid_ref[...] = (act * u).T.astype(BF16)

    return pl.pallas_call(
        body,
        grid_spec=pltpu.PrefetchScalarGridSpec(
            num_scalar_prefetch=1,
            grid=(pl.cdiv(hidden, hb),),
            in_specs=[whole(a.shape) for a in (*own, *other)]
            + [pl.BlockSpec((hb, model), lambda k, s: (k, 0))] * 2,
            out_specs=[
                pl.BlockSpec((m, hb), lambda k, s: (0, k)),
                pl.BlockSpec((m, hb), lambda k, s: (0, k)),
                pl.BlockSpec((hb, m), lambda k, s: (k, 0)),
            ],
            scratch_shapes=[pltpu.VMEM((m, half), BF16)] * 2,
        ),
        out_shape=[
            jax.ShapeDtypeStruct((m, hidden), F32),
            jax.ShapeDtypeStruct((m, hidden), F32),
            jax.ShapeDtypeStruct((hidden, m), BF16),
        ],
        compiler_params=params(),
        cost_estimate=cost(4 * m * model * hidden, 4 * model * hidden),
        name="gate_up",
    )(info, *own, *other, w_gate, w_up)


def hidden_grads(info, own, other, w_down, act, dact, row0, hb=512):
    hidden, model = w_down.shape
    half = model // 2
    sizes = [a.shape[0] for a in own]
    m, n = sum(sizes), len(own)
    full = act.shape[0]

    def body(s, *refs):
        xo, xt = refs[:n], refs[n : 2 * n]
        w_ref, a_ref, da_ref, ug_ref, gg_ref, xa, xb = refs[2 * n :]

        @pl.when(pl.program_id(0) == 0)
        def _():
            at = 0
            for i, rows in enumerate(sizes):
                xa[at : at + rows] = xo[i][...]
                xb[at : at + rows] = xt[i][...]
                at += rows

        mine = pl.ds(pl.multiple_of(s[1] * half, 128), half)
        others = pl.ds(pl.multiple_of((1 - s[1]) * half, 128), half)
        h = lax.dot_general(xa[...], w_ref[:, mine], NT, preferred_element_type=F32)
        h = h + lax.dot_general(xb[...], w_ref[:, others], NT, preferred_element_type=F32)
        ug_ref[...] = (h * a_ref[row0 : row0 + m]).astype(BF16)
        gg_ref[...] = (h * da_ref[row0 : row0 + m]).astype(BF16)

    return pl.pallas_call(
        body,
        grid_spec=pltpu.PrefetchScalarGridSpec(
            num_scalar_prefetch=1,
            grid=(pl.cdiv(hidden, hb),),
            in_specs=[whole(a.shape) for a in (*own, *other)]
            + [pl.BlockSpec((hb, model), lambda k, s: (k, 0))]
            + [pl.BlockSpec((full, hb), lambda k, s: (0, k))] * 2,
            out_specs=[pl.BlockSpec((m, hb), lambda k, s: (0, k))] * 2,
            scratch_shapes=[pltpu.VMEM((m, half), BF16)] * 2,
        ),
        out_shape=[jax.ShapeDtypeStruct((m, hidden), BF16)] * 2,
        compiler_params=params(),
        cost_estimate=cost(2 * m * model * hidden, 2 * model * hidden),
        name="hidden_grads",
    )(info, *own, *other, w_down, act, dact)


def partial_half(info, gate_grad, up_grad, w_gate, w_up, kept, db=1024):
    hidden, model = w_gate.shape
    half = model // 2
    db = min(db, half)
    steps = half // db
    m = gate_grad.shape[0]

    def column(k, s):
        side = s[1] if kept else 1 - s[1]
        return (0, side * steps + k)

    def body(s, g_ref, u_ref, wg_ref, wu_ref, o_ref):
        o = jnp.dot(g_ref[...], wg_ref[...], preferred_element_type=F32)
        o = o + jnp.dot(u_ref[...], wu_ref[...], preferred_element_type=F32)
        o_ref[...] = o.astype(BF16)

    return pl.pallas_call(
        body,
        grid_spec=pltpu.PrefetchScalarGridSpec(
            num_scalar_prefetch=1,
            grid=(steps,),
            in_specs=[whole((m, hidden))] * 2 + [pl.BlockSpec((hidden, db), column)] * 2,
            out_specs=pl.BlockSpec((m, db), lambda k, s: (0, k)),
        ),
        out_shape=jax.ShapeDtypeStruct((m, half), BF16),
        compiler_params=params(),
        cost_estimate=cost(4 * m * half * hidden, 4 * half * hidden),
        name="partial",
    )(info, gate_grad, up_grad, w_gate, w_up)


def down_grads(info, hidden_t, own, other, db=1024):
    hidden, m = hidden_t.shape
    half = own[0].shape[1]
    db = min(db, half)
    steps = half // db
    sizes = [a.shape[0] for a in own]
    n = len(own)

    def body(s, h_ref, *refs):
        go, gt, o_ref, g = refs[:n], refs[n : 2 * n], refs[2 * n], refs[2 * n + 1]

        def fill(parts):
            at = 0
            for i, rows in enumerate(sizes):
                g[at : at + rows] = parts[i][...]
                at += rows

        @pl.when(pl.program_id(0) < steps)
        def _():
            fill(go)

        @pl.when(pl.program_id(0) >= steps)
        def _():
            fill(gt)

        o_ref[...] = jnp.dot(h_ref[...], g[...], preferred_element_type=F32).astype(BF16)

    return pl.pallas_call(
        body,
        grid_spec=pltpu.PrefetchScalarGridSpec(
            num_scalar_prefetch=1,
            grid=(2 * steps,),
            in_specs=[whole(hidden_t.shape)]
            + [pl.BlockSpec((r, db), lambda k, s: (0, jnp.minimum(k, steps - 1))) for r in sizes]
            + [pl.BlockSpec((r, db), lambda k, s: (0, jnp.maximum(k - steps, 0))) for r in sizes],
            out_specs=pl.BlockSpec(
                (hidden, db), lambda k, s: (0, lax.rem(k + s[1] * steps, 2 * steps))
            ),
            scratch_shapes=[pltpu.VMEM((m, db), BF16)],
        ),
        out_shape=jax.ShapeDtypeStruct((hidden, 2 * half), BF16),
        compiler_params=params(),
        cost_estimate=cost(4 * m * half * hidden, 4 * half * hidden),
        name="down_grads",
    )(info, hidden_t, *own, *other)


GROUPS = ((0,), (1, 3), (2,))
CHUNKS = ((0, 2), (1,))


def shards(tokens, token_grad_in, expert_ids, gate_weight, up_weight, down_weight):
    devices = lax.axis_size("expert")
    rows, model = tokens.shape
    half = model // 2
    share = devices // EXPERTS
    capacity = (rows + EXPERTS) // (EXPERTS + 1) + 1
    slots = -(-2 * capacity // 8) * 8
    bits = [b for b in range(1, share.bit_length() - 1)]
    index = lax.axis_index("expert")
    core = lax.rem(index, 2)
    info = jnp.stack([index // share, core]).astype(jnp.int32)

    def flip(x, bit):
        return lax.ppermute(x, "expert", [(i, i ^ (1 << bit)) for i in range(devices)])

    def plane_shift(x, d):
        return lax.ppermute(
            x, "expert", [(i, (i + d * share) % devices) for i in range(devices)]
        )

    def split(x):
        mine = lax.dynamic_slice_in_dim(x, core * half, half, 1)
        others = lax.dynamic_slice_in_dim(x, (1 - core) * half, half, 1)
        return mine, flip(others, 0)

    other_ids = flip(expert_ids, 0)

    def forward(x):
        mine, other = split(x)
        pieces = pack(info, expert_ids, other_ids, mine, other, slots, capacity)
        pieces = [pieces[0]] + [plane_shift(pieces[d], d) for d in range(1, EXPERTS)]
        own, others = [], []
        for group in GROUPS:
            part = jnp.concatenate([pieces[d] for d in group], axis=0)
            for bit in bits:
                part = jnp.concatenate([part, flip(part, bit)], axis=0)
            own.append(part)
            others.append(flip(part, 0))
        return own, others

    w_gate = jnp.swapaxes(gate_weight[0], 0, 1)
    w_up = jnp.swapaxes(up_weight[0], 0, 1)
    w_down = down_weight[0]

    x_own, x_other = forward(tokens)
    g_own, g_other = forward(token_grad_in)
    sizes = [a.shape[0] for a in x_own]
    order = [g for chunk in CHUNKS for g in chunk]
    act, dact, hidden_t = gate_up(
        info, [x_own[g] for g in order], [x_other[g] for g in order], w_gate, w_up
    )
    pieces = {}
    row0 = 0
    for chunk in CHUNKS:
        up_grad, gate_grad = hidden_grads(
            info, [g_own[g] for g in chunk], [g_other[g] for g in chunk], w_down, act, dact, row0
        )
        row0 += sum(sizes[g] for g in chunk)
        sent = flip(partial_half(info, gate_grad, up_grad, w_gate, w_up, 0), 0)
        kept = partial_half(info, gate_grad, up_grad, w_gate, w_up, 1)
        at = 0
        for g in chunk:
            total = kept[at : at + sizes[g]].astype(F32) + sent[at : at + sizes[g]].astype(F32)
            at += sizes[g]
            for bit in reversed(bits):
                mid = total.shape[0] // 2
                total = total[:mid] + flip(total[mid:].astype(BF16), bit).astype(F32)
            for i, d in enumerate(GROUPS[g]):
                piece = total[i * slots : (i + 1) * slots].astype(BF16)
                pieces[d] = plane_shift(piece, EXPERTS - d) if d else piece
    down_grad = down_grads(
        info, hidden_t, [g_own[g] for g in order], [g_other[g] for g in order]
    )
    mine, theirs = unpack(
        info, expert_ids, other_ids, [pieces[d] for d in range(EXPERTS)], slots, capacity
    )
    got = flip(theirs, 0)
    input_grad = jnp.where(
        core == 0,
        jnp.concatenate([mine, got], axis=1),
        jnp.concatenate([got, mine], axis=1),
    )
    return (input_grad, down_grad[None])


def solution(mesh):
    placed = (
        P(("groups", "expert"), None),
        P(("groups", "expert"), None),
        P(("groups", "expert"), None),
        P("expert", None, None),
        P("expert", None, None),
        P("expert", None, None),
    )
    return jax.shard_map(
        shards,
        mesh=mesh,
        in_specs=placed,
        out_specs=(P(("groups", "expert"), None), P(("groups", "expert"), None, None)),
        check_vma=False,
    )
```

```python
import jax
import jax.numpy as jnp
from jax import lax
from jax.experimental import pallas as pl
from jax.experimental.pallas import tpu as pltpu
from jax.sharding import PartitionSpec as P

EXPERTS = 4
F32, BF16 = jnp.float32, jnp.bfloat16
NT = (((1,), (1,)), ((), ()))
TN = (((0,), (0,)), ((), ()))
MIB = 1024 * 1024
HBLOCK = 512
LIMIT = 12


def limit(rows):
    return LIMIT if rows <= 448 else 28


def cost(flops, nbytes):
    return pl.CostEstimate(flops=flops, bytes_accessed=nbytes, transcendentals=0)


def on_core(body, info, args, outs, name, flops, limit, deps=(), scratch=(), far=(), hbm=0):
    if hbm:
        args = (*args[:-hbm], *[in_hbm(x) for x in args[-hbm:]])
    n, d = len(args), len(deps) + len(far)

    def run(s, *refs):
        body(s, refs[:n], refs[n + d : n + d + len(outs)], refs[n + d + len(outs) :])

    vmem = pl.BlockSpec(memory_space=pltpu.VMEM)
    nbytes = sum(a.size * a.dtype.itemsize for a in args)
    return pl.pallas_call(
        run,
        in_specs=[pl.BlockSpec(memory_space=pltpu.SMEM)]
        + [vmem] * (n - hbm)
        + [pl.BlockSpec(memory_space=pltpu.HBM)] * hbm
        + [pl.BlockSpec(memory_space=pl.ANY)] * len(deps)
        + [pl.BlockSpec(memory_space=pltpu.HBM)] * len(far),
        out_specs=[vmem] * len(outs),
        out_shape=outs,
        scratch_shapes=scratch,
        compiler_params=pltpu.CompilerParams(vmem_limit_bytes=limit * MIB),
        cost_estimate=cost(flops, nbytes),
        name=name,
    )(info, *args, *deps, *[in_hbm(x) for x in far])


def slot_map(ids, plane, slots, which, capacity):
    rows = ids.shape[0]
    lane = lax.broadcasted_iota(jnp.int32, (rows, 128), 1)
    onehot = jnp.where(ids == lane, 1.0, 0.0)
    row_i = lax.broadcasted_iota(jnp.int32, (rows, rows), 0)
    col_i = lax.broadcasted_iota(jnp.int32, (rows, rows), 1)
    earlier = jnp.where(col_i < row_i, 1.0, 0.0).astype(BF16)
    before = jnp.dot(earlier, onehot.astype(BF16), preferred_element_type=F32)
    slot = jnp.sum(before * onehot, axis=1, keepdims=True).astype(jnp.int32)
    shift = ids - plane
    shift = jnp.where(shift < 0, shift + EXPERTS, shift)
    target = shift * slots + which * capacity + slot
    target = jnp.where(ids < EXPERTS, target, -1)
    place = lax.broadcasted_iota(jnp.int32, (rows, EXPERTS * slots), 1)
    return jnp.where(target == place, 1.0, 0.0).astype(BF16)


def side(s, half, mine):
    return pl.ds(pl.multiple_of((s[1] if mine else 1 - s[1]) * half, 128), half)


def pack(info, ids, other_ids, tokens, grads, received, slots, capacity):
    rows, half = tokens.shape

    def body(s, refs, outs, _):
        ids_ref, oids_ref, tok_ref, grad_ref, got_ref = refs
        p = slot_map(ids_ref[...], s[0], slots, s[1], capacity)
        q = slot_map(oids_ref[...], s[0], slots, 1 - s[1], capacity)
        for i, ref in enumerate((tok_ref, grad_ref)):
            got = lax.dot_general(p, ref[...], TN, preferred_element_type=F32)
            got = got + lax.dot_general(
                q, got_ref[i * rows : (i + 1) * rows], TN, preferred_element_type=F32
            )
            got = got.astype(BF16)
            for d in range(EXPERTS):
                outs[i * EXPERTS + d][...] = got[d * slots : (d + 1) * slots]

    outs = [jax.ShapeDtypeStruct((slots, half), BF16)] * (2 * EXPERTS)
    args = (ids, other_ids, tokens, grads, received)
    made = on_core(body, info, args, outs, "pack", 8 * rows * 4 * slots * half, LIMIT)
    return made[:EXPERTS], made[EXPERTS:]


def unpack(info, ids, other_ids, pieces, slots, capacity, deps):
    rows, width = ids.shape[0], pieces[0].shape[1]

    def body(s, refs, outs, _):
        p = slot_map(refs[0][...], s[0], slots, s[1], capacity)
        q = slot_map(refs[1][...], s[0], slots, 1 - s[1], capacity)
        z = jnp.concatenate([r[...].astype(F32) for r in refs[2:]], axis=0).astype(BF16)
        outs[0][...] = jnp.dot(p, z, preferred_element_type=F32).astype(BF16)
        outs[1][...] = jnp.dot(q, z, preferred_element_type=F32).astype(BF16)

    outs = [jax.ShapeDtypeStruct((rows, width), BF16)] * 2
    args = (ids, other_ids, *pieces)
    flops = 4 * rows * EXPERTS * slots * width
    return on_core(body, info, args, outs, "unpack", flops, LIMIT, (), (), deps)


def stack(to, refs, parts):
    at = 0
    for which, row, rows in parts:
        to[at : at + rows] = refs[which][row : row + rows]
        at += rows


def join(info, arrays, parts, deps=()):
    def body(s, refs, outs, _):
        stack(outs[0], refs, parts)

    rows, width = sum(p[2] for p in parts), arrays[0].shape[1]
    outs = [jax.ShapeDtypeStruct((rows, width), arrays[0].dtype)]
    return on_core(body, info, arrays, outs, "join", 0, LIMIT, deps)[0]


def joined(info, arrays, deps=()):
    return join(info, arrays, [(i, 0, a.shape[0]) for i, a in enumerate(arrays)], deps)


def add_split(info, a, b, parts):
    rows, width = sum(p[2] for p in parts), a.shape[1]
    mid = rows // 2
    each = min(mid, min(p[2] for p in parts))
    pieces = [(row + i, each) for _, row, n in parts for i in range(0, n, each)]

    def body(s, refs, outs, _):
        x, y = refs
        for i, (row, n) in enumerate(pieces):
            cut, at = slice(row, row + n), i * each
            total = x[cut].astype(F32) + y[cut].astype(F32)
            if at < mid:
                outs[1][at : at + n] = total
            else:
                outs[0][at - mid : at - mid + n] = total.astype(BF16)

    outs = [
        jax.ShapeDtypeStruct((rows - mid, width), BF16),
        jax.ShapeDtypeStruct((mid, width), F32),
    ]
    return on_core(body, info, (a, b), outs, "add_split", 2 * a.size, LIMIT)


def add_pieces(info, a, b, count, deps=()):
    rows, width = a.shape
    each = rows // count

    def body(s, refs, outs, _):
        for i, out in enumerate(outs):
            cut = slice(i * each, (i + 1) * each)
            out[...] = (refs[0][cut].astype(F32) + refs[1][cut].astype(F32)).astype(BF16)

    outs = [jax.ShapeDtypeStruct((each, width), BF16)] * count
    return on_core(body, info, (a, b), outs, "add_pieces", 2 * a.size, LIMIT, deps)


def in_vmem(x):
    return pltpu.with_memory_space_constraint(x, pltpu.VMEM)


def in_hbm(x):
    return pltpu.with_memory_space_constraint(x, pltpu.HBM)


def load(info, w, name, deps=()):
    def body(s, w_ref, *rest):
        out_ref, sem = rest[-2:]
        copy = pltpu.make_async_copy(w_ref, out_ref, sem)
        copy.start()
        copy.wait()

    return pl.pallas_call(
        body,
        in_specs=[pl.BlockSpec(memory_space=pltpu.SMEM)]
        + [pl.BlockSpec(memory_space=pltpu.HBM)]
        + [pl.BlockSpec(memory_space=pl.ANY)] * len(deps),
        out_specs=pl.BlockSpec(memory_space=pltpu.VMEM),
        out_shape=pltpu.VMEM(w.shape, w.dtype),
        scratch_shapes=[pltpu.SemaphoreType.DMA],
        compiler_params=pltpu.CompilerParams(vmem_limit_bytes=LIMIT * MIB),
        cost_estimate=cost(0, 2 * w.size * 2),
        name=name,
    )(info, in_hbm(w), *deps)


def cuts_of(size, step):
    return [(at, min(at + step, size)) for at in range(0, size, step)]


def wide_dot(s, own, other, w_ref, cut):
    half = own.shape[1]
    return lax.dot_general(
        own, w_ref[cut, side(s, half, True)], NT, preferred_element_type=F32
    ) + lax.dot_general(other, w_ref[cut, side(s, half, False)], NT, preferred_element_type=F32)


def gate_up(info, own, other, w_gate, w_up, deps=()):
    hidden, model = w_gate.shape
    m = own.shape[0]

    def body(s, refs, outs, _):
        own_ref, other_ref, g_ref, u_ref = refs
        act_ref, dact_ref, hid_ref = outs
        for at, to in cuts_of(hidden, HBLOCK):
            cut = slice(at, to)
            g = wide_dot(s, own_ref[...], other_ref[...], g_ref, cut)
            u = wide_dot(s, own_ref[...], other_ref[...], u_ref, cut)
            sig = jax.nn.sigmoid(g)
            act = g * sig
            act_ref[:, cut] = act
            dact_ref[:, cut] = u * sig * (1.0 + g * (1.0 - sig))
            hid_ref[:, cut] = (act * u).astype(BF16)

    outs = [
        jax.ShapeDtypeStruct((m, hidden), F32),
        jax.ShapeDtypeStruct((m, hidden), F32),
        jax.ShapeDtypeStruct((m, hidden), BF16),
    ]
    args = (own, other, in_vmem(w_gate), in_vmem(w_up))
    return on_core(body, info, args, outs, "gate_up", 4 * m * model * hidden, limit(m), deps)


def hidden_grads(info, own, other, act, dact, w_down, far=()):
    hidden, model = w_down.shape
    m = own.shape[0]
    cuts = cuts_of(hidden, HBLOCK)

    def body(s, refs, outs, scratch):
        own_ref, other_ref, act_ref, dact_ref, d_hbm = refs
        ug_ref, gg_ref = outs
        d_ref, sem = scratch
        copies = [
            pltpu.make_async_copy(
                d_hbm.at[pl.ds(at, to - at)], d_ref.at[j % 2, pl.ds(0, to - at)], sem.at[j]
            )
            for j, (at, to) in enumerate(cuts)
        ]
        for copy in copies[:2]:
            copy.start()
        for j, (at, to) in enumerate(cuts):
            copies[j].wait()
            h = wide_dot(s, own_ref[...], other_ref[...], d_ref.at[j % 2], slice(0, to - at))
            if j + 2 < len(cuts):
                copies[j + 2].start()
            ug_ref[:, at:to] = (h * act_ref[:, at:to]).astype(BF16)
            gg_ref[:, at:to] = (h * dact_ref[:, at:to]).astype(BF16)

    outs = [jax.ShapeDtypeStruct((m, hidden), BF16)] * 2
    args = (own, other, act, dact, w_down)
    scratch = [
        pltpu.VMEM((2, HBLOCK, model), BF16),
        pltpu.SemaphoreType.DMA((len(cuts),)),
    ]
    flops = 2 * m * model * hidden
    return on_core(body, info, args, outs, "hidden_grads", flops, limit(m), (), scratch, far, 1)


def partial(info, up_grad, gate_grad, row0, m, w_gate, w_up, mine, deps=()):
    hidden, model = w_gate.shape
    half = model // 2

    def body(s, refs, outs, _):
        ug_ref, gg_ref, g_ref, u_ref = refs
        rows = slice(row0, row0 + m)
        o = jnp.dot(gg_ref[rows], g_ref[:, side(s, half, mine)], preferred_element_type=F32)
        o = o + jnp.dot(ug_ref[rows], u_ref[:, side(s, half, mine)], preferred_element_type=F32)
        outs[0][...] = o.astype(BF16)

    outs = [jax.ShapeDtypeStruct((m, half), BF16)]
    args = (up_grad, gate_grad, in_vmem(w_gate), in_vmem(w_up))
    flops = 4 * m * half * hidden
    return on_core(body, info, args, outs, "partial", flops, LIMIT, deps)[0]


def down_grads(info, hid, g, mine, filled=None, deps=(), db=1024):
    m, hidden = hid.shape
    half = g.shape[1]
    db = min(db, half)
    steps = half // db

    def column(k, s):
        return (0, k + (s[1] if mine else 1 - s[1]) * steps)

    def body(s, h_ref, g_ref, *refs):
        o = lax.dot_general(h_ref[...], g_ref[...], TN, preferred_element_type=F32)
        refs[-1][...] = o.astype(BF16)

    old = [] if filled is None else [in_hbm(filled)]
    return pl.pallas_call(
        body,
        grid_spec=pltpu.PrefetchScalarGridSpec(
            num_scalar_prefetch=1,
            grid=(steps,),
            in_specs=[pl.BlockSpec((m, hidden), lambda k, s: (0, 0))]
            + [pl.BlockSpec((m, db), lambda k, s: (0, k))]
            + [pl.BlockSpec(memory_space=pltpu.HBM)] * len(old)
            + [pl.BlockSpec(memory_space=pl.ANY)] * len(deps),
            out_specs=pl.BlockSpec((hidden, db), column),
        ),
        out_shape=jax.ShapeDtypeStruct((hidden, 2 * half), BF16),
        input_output_aliases={3: 0} if old else {},
        compiler_params=pltpu.CompilerParams(vmem_limit_bytes=limit(m) * MIB),
        cost_estimate=cost(2 * m * half * hidden, 2 * half * hidden),
        name="down_grads",
    )(info, hid, g, *old, *deps)


def shards(tokens, token_grad_in, expert_ids, gate_weight, up_weight, down_weight):
    devices = lax.axis_size("expert")
    rows, model = tokens.shape
    half = model // 2
    share = devices // EXPERTS
    capacity = (rows + EXPERTS) // (EXPERTS + 1) + 1
    slots = -(-2 * capacity // 8) * 8
    bits = [b for b in range(1, share.bit_length() - 1)]
    index = lax.axis_index("expert")
    core = lax.rem(index, 2)
    info = jnp.stack([index // share, core]).astype(jnp.int32)

    def flip(x, bit):
        return lax.ppermute(x, "expert", [(i, i ^ (1 << bit)) for i in range(devices)])

    def plane_shift(x, d):
        return lax.ppermute(
            x, "expert", [(i, (i + d * share) % devices) for i in range(devices)]
        )

    def after(x, *others):
        return lax.optimization_barrier((x, *others))[0]

    def spread(parts):
        for bit in bits:
            parts = parts + [flip(p, bit) for p in parts]
        return parts

    def fold(halves):
        for i, bit in enumerate(reversed(bits)):
            out, kept = halves
            got = flip(out, bit)
            if i + 1 < len(bits):
                halves = add_split(info, kept, got, [(0, 0, kept.shape[0])])
        return add_pieces(info, kept, got, 1)[0]

    w_gate = jnp.swapaxes(gate_weight[0], 0, 1)
    w_up = jnp.swapaxes(up_weight[0], 0, 1)
    w_down = down_weight[0]

    away, here = (1 - core) * half, core * half
    sent = jnp.concatenate(
        [
            lax.dynamic_slice_in_dim(tokens, away, half, 1),
            lax.dynamic_slice_in_dim(token_grad_in, away, half, 1),
        ],
        axis=0,
    )
    received = flip(sent, 0)
    other_ids = flip(expert_ids, 0)
    tok, grad = pack(
        info,
        expert_ids,
        other_ids,
        lax.dynamic_slice_in_dim(tokens, here, half, 1),
        lax.dynamic_slice_in_dim(token_grad_in, here, half, 1),
        received,
        slots,
        capacity,
    )

    t1, t3, t2 = plane_shift(tok[1], 1), plane_shift(tok[3], 3), plane_shift(tok[2], 2)
    near = spread([joined(info, [tok[0], grad[0]])])
    w_gate = load(info, w_gate, "load_gate", (tok[0],))
    w_up = load(info, w_up, "load_up", (tok[0],))
    chips = len(near)
    n = chips * slots

    def by_plane(x, near_row, deps):
        rows = [(c, near_row, slots) for c in range(chips)]
        rows += [(chips + c, i * slots, slots) for i in range(3) for c in range(chips)]
        return join(info, [*near, *x], rows, deps)

    t = joined(info, [t2, t1, t3], (w_gate, w_up, *near))
    g2 = plane_shift(after(grad[2], t), 2)
    g1 = plane_shift(after(grad[1], t), 1)
    g3 = plane_shift(after(grad[3], t), 3)
    t = by_plane(spread([t]), 0, (g1, g2, g3))
    t_other = flip(t, 0)
    g = spread([joined(info, [g2, g1, g3], (t,))])
    act, dact, hid = gate_up(info, t, t_other, w_gate, w_up)
    g = by_plane(g, slots, (hid,))
    g_other = flip(g, 0)
    down_grad = down_grads(info, hid, g, True)
    up_grad, gate_grad = hidden_grads(info, g, g_other, act, dact, w_down, (down_grad,))

    def back(row0, mine, deps=()):
        return partial(info, up_grad, gate_grad, row0, 2 * n, w_gate, w_up, mine, deps)

    def plane(i):
        return [(0, i * n, n)]

    got = flip(back(0, False), 0)
    kept = back(0, True)
    sum2 = add_split(info, kept, got, plane(1))
    sum0 = add_split(info, kept, got, plane(0))
    got = flip(back(2 * n, False, (sum2[0],)), 0)
    far2 = fold(sum2)
    piece2 = plane_shift(far2, EXPERTS - 2)
    kept = back(2 * n, True)
    sum1 = add_split(info, kept, got, plane(0))
    sum3 = add_split(info, kept, got, plane(1))
    piece1 = plane_shift(fold(sum1), EXPERTS - 1)
    down_grad = down_grads(info, hid, g_other, False, down_grad, (sum3[0], far2))
    piece3 = plane_shift(fold(sum3), EXPERTS - 3)
    piece0 = fold(sum0)
    pieces = {0: piece0, 1: piece1, 2: piece2, 3: piece3}
    mine, theirs = unpack(
        info,
        expert_ids,
        other_ids,
        [pieces[d] for d in range(EXPERTS)],
        slots,
        capacity,
        (down_grad,),
    )
    got = flip(theirs, 0)
    input_grad = jnp.where(
        core == 0,
        jnp.concatenate([mine, got], axis=1),
        jnp.concatenate([got, mine], axis=1),
    )
    return (input_grad, down_grad[None])


def solution(mesh):
    placed = (
        P(("groups", "expert"), None),
        P(("groups", "expert"), None),
        P(("groups", "expert"), None),
        P("expert", None, None),
        P("expert", None, None),
        P("expert", None, None),
    )
    return jax.shard_map(
        shards,
        mesh=mesh,
        in_specs=placed,
        out_specs=(P(("groups", "expert"), None), P(("groups", "expert"), None, None)),
        check_vma=False,
    )
```

```python
import jax
import jax.numpy as jnp
from jax import lax
from jax.experimental import pallas as pl
from jax.experimental.pallas import tpu as pltpu
from jax.sharding import PartitionSpec as P

EXPERTS = 4
F32, BF16 = jnp.float32, jnp.bfloat16
NT = (((1,), (1,)), ((), ()))
TN = (((0,), (0,)), ((), ()))
MIB = 1024 * 1024
HBLOCK = 512
LIMIT = 8


def limit(rows):
    return LIMIT if rows <= 448 else 28


def cost(flops, nbytes):
    return pl.CostEstimate(flops=flops, bytes_accessed=nbytes, transcendentals=0)


def on_core(body, info, args, outs, name, flops, limit, deps=(), scratch=(), far=(), hbm=0):
    if hbm:
        args = (*args[:-hbm], *[in_hbm(x) for x in args[-hbm:]])
    n, d = len(args), len(deps) + len(far)

    def run(s, *refs):
        body(s, refs[:n], refs[n + d : n + d + len(outs)], refs[n + d + len(outs) :])

    vmem = pl.BlockSpec(memory_space=pltpu.VMEM)
    nbytes = sum(a.size * a.dtype.itemsize for a in args) if flops else 1
    return pl.pallas_call(
        run,
        in_specs=[pl.BlockSpec(memory_space=pltpu.SMEM)]
        + [vmem] * (n - hbm)
        + [pl.BlockSpec(memory_space=pltpu.HBM)] * hbm
        + [pl.BlockSpec(memory_space=pl.ANY)] * len(deps)
        + [pl.BlockSpec(memory_space=pltpu.HBM)] * len(far),
        out_specs=[vmem] * len(outs),
        out_shape=outs,
        scratch_shapes=scratch,
        compiler_params=pltpu.CompilerParams(vmem_limit_bytes=limit * MIB),
        cost_estimate=cost(flops, nbytes),
        name=name,
    )(info, *args, *deps, *[in_hbm(x) for x in far])


def slot_map(ids, plane, slots, which, capacity):
    rows = ids.shape[0]
    lane = lax.broadcasted_iota(jnp.int32, (rows, 128), 1)
    onehot = jnp.where(ids == lane, 1.0, 0.0)
    row_i = lax.broadcasted_iota(jnp.int32, (rows, rows), 0)
    col_i = lax.broadcasted_iota(jnp.int32, (rows, rows), 1)
    earlier = jnp.where(col_i < row_i, 1.0, 0.0).astype(BF16)
    before = jnp.dot(earlier, onehot.astype(BF16), preferred_element_type=F32)
    slot = jnp.sum(before * onehot, axis=1, keepdims=True).astype(jnp.int32)
    shift = ids - plane
    shift = jnp.where(shift < 0, shift + EXPERTS, shift)
    target = shift * slots + which * capacity + slot
    target = jnp.where(ids < EXPERTS, target, -1)
    place = lax.broadcasted_iota(jnp.int32, (rows, EXPERTS * slots), 1)
    return jnp.where(target == place, 1.0, 0.0).astype(BF16)


def side(s, half, mine):
    return pl.ds(pl.multiple_of((s[1] if mine else 1 - s[1]) * half, 128), half)


def halves(info, tokens, grads):
    rows, model = tokens.shape
    half = model // 2

    def body(s, refs, outs, scratch):
        copies = [
            pltpu.make_async_copy(
                ref.at[:, side(s, half, mine)],
                outs[0 if mine else 1].at[pl.ds(i * rows, rows)],
                scratch[0].at[2 * i + mine],
            )
            for i, ref in enumerate(refs)
            for mine in (False, True)
        ]
        for copy in copies:
            copy.start()
        for copy in copies:
            copy.wait()

    outs = [jax.ShapeDtypeStruct((2 * rows, half), BF16)] * 2
    scratch = [pltpu.SemaphoreType.DMA((4,))]
    return on_core(body, info, (tokens, grads), outs, "halves", 0, LIMIT, (), scratch, (), 2)


def pack(info, ids, other_ids, mine, received, slots, capacity):
    rows, half = mine.shape[0] // 2, mine.shape[1]

    def body(s, refs, outs, _):
        ids_ref, oids_ref, mine_ref, got_ref = refs
        p = slot_map(ids_ref[...], s[0], slots, s[1], capacity)
        q = slot_map(oids_ref[...], s[0], slots, 1 - s[1], capacity)
        for i in range(2):
            cut = slice(i * rows, (i + 1) * rows)
            got = lax.dot_general(p, mine_ref[cut], TN, preferred_element_type=F32)
            got = got + lax.dot_general(q, got_ref[cut], TN, preferred_element_type=F32)
            got = got.astype(BF16)
            outs[0][i * slots : (i + 1) * slots] = got[:slots]
            for d in range(1, EXPERTS):
                outs[i * (EXPERTS - 1) + d][...] = got[d * slots : (d + 1) * slots]

    outs = [jax.ShapeDtypeStruct((2 * slots, half), BF16)]
    outs += [jax.ShapeDtypeStruct((slots, half), BF16)] * (2 * EXPERTS - 2)
    args = (ids, other_ids, mine, received)
    made = on_core(body, info, args, outs, "pack", 8 * rows * 4 * slots * half, LIMIT)
    return made[0], (None, *made[1:EXPERTS]), (None, *made[EXPERTS:])


def unpack(info, ids, other_ids, pieces, slots, capacity, deps):
    rows, width = ids.shape[0], pieces[0].shape[1]

    def body(s, refs, outs, _):
        p = slot_map(refs[0][...], s[0], slots, s[1], capacity)
        q = slot_map(refs[1][...], s[0], slots, 1 - s[1], capacity)
        z = jnp.concatenate([r[...].astype(F32) for r in refs[2:]], axis=0).astype(BF16)
        outs[0][...] = jnp.dot(p, z, preferred_element_type=F32).astype(BF16)
        outs[1][...] = jnp.dot(q, z, preferred_element_type=F32).astype(BF16)

    outs = [jax.ShapeDtypeStruct((rows, width), BF16)] * 2
    args = (ids, other_ids, *pieces)
    flops = 4 * rows * EXPERTS * slots * width
    return on_core(body, info, args, outs, "unpack", flops, LIMIT, (), (), deps)


def stack(to, refs, parts):
    at = 0
    for which, row, rows in parts:
        to[at : at + rows] = refs[which][row : row + rows]
        at += rows


def join(info, arrays, parts, deps=()):
    def body(s, refs, outs, _):
        stack(outs[0], refs, parts)

    rows, width = sum(p[2] for p in parts), arrays[0].shape[1]
    outs = [jax.ShapeDtypeStruct((rows, width), arrays[0].dtype)]
    return on_core(body, info, arrays, outs, "join", 0, LIMIT, deps)[0]


def joined(info, arrays, deps=()):
    return join(info, arrays, [(i, 0, a.shape[0]) for i, a in enumerate(arrays)], deps)


def add_split(info, a, b, parts, deps=()):
    rows, width = sum(p[1] for p in parts), a.shape[1]
    mid, size = rows // 2, b[0].shape[0]
    each = min(mid, size, min(p[1] for p in parts))
    pieces = [row + i for row, n in parts for i in range(0, n, each)]

    def body(s, refs, outs, _):
        for i, row in enumerate(pieces):
            at, y = i * each, refs[1 + row // size]
            total = refs[0][row : row + each].astype(F32)
            total = total + y[row % size : row % size + each].astype(F32)
            if at < mid:
                outs[1][at : at + each] = total
            else:
                outs[0][at - mid : at - mid + each] = total.astype(BF16)

    outs = [
        jax.ShapeDtypeStruct((rows - mid, width), BF16),
        jax.ShapeDtypeStruct((mid, width), F32),
    ]
    return on_core(body, info, (a, *b), outs, "add_split", 0, LIMIT, deps)


def add_rounded(info, a, b, count, deps=(), far=()):
    each = a.shape[0] // count

    def body(s, refs, outs, _):
        for i, out in enumerate(outs):
            cut = slice(i * each, (i + 1) * each)
            out[...] = (refs[0][cut].astype(F32) + refs[1][cut].astype(F32)).astype(BF16)

    outs = [jax.ShapeDtypeStruct((each, a.shape[1]), BF16)] * count
    return on_core(body, info, (a, b), outs, "add_rounded", 0, LIMIT, deps, (), far)


def in_vmem(x):
    return pltpu.with_memory_space_constraint(x, pltpu.VMEM)


def in_hbm(x):
    return pltpu.with_memory_space_constraint(x, pltpu.HBM)


def load(info, w, name, deps=()):
    def body(s, w_ref, *rest):
        out_ref, sem = rest[-2:]
        copy = pltpu.make_async_copy(w_ref, out_ref, sem)
        copy.start()
        copy.wait()

    return pl.pallas_call(
        body,
        in_specs=[pl.BlockSpec(memory_space=pltpu.SMEM)]
        + [pl.BlockSpec(memory_space=pltpu.HBM)]
        + [pl.BlockSpec(memory_space=pl.ANY)] * len(deps),
        out_specs=pl.BlockSpec(memory_space=pltpu.VMEM),
        out_shape=pltpu.VMEM(w.shape, w.dtype),
        scratch_shapes=[pltpu.SemaphoreType.DMA],
        compiler_params=pltpu.CompilerParams(vmem_limit_bytes=LIMIT * MIB),
        cost_estimate=cost(0, 2 * w.size * 2),
        name=name,
    )(info, in_hbm(w), *deps)


def cuts_of(size, step):
    return [(at, min(at + step, size)) for at in range(0, size, step)]


def wide_dot(s, own, other, w_ref, cut):
    half = own.shape[1]
    return lax.dot_general(
        own, w_ref[cut, side(s, half, True)], NT, preferred_element_type=F32
    ) + lax.dot_general(other, w_ref[cut, side(s, half, False)], NT, preferred_element_type=F32)


def gate_up(info, own, other, w_gate, w_up, deps=()):
    hidden, model = w_gate.shape
    m = own.shape[0]

    def body(s, refs, outs, _):
        own_ref, other_ref, g_ref, u_ref = refs
        act_ref, dact_ref, hid_ref = outs
        for at, to in cuts_of(hidden, HBLOCK):
            cut = slice(at, to)
            g = wide_dot(s, own_ref[...], other_ref[...], g_ref, cut)
            u = wide_dot(s, own_ref[...], other_ref[...], u_ref, cut)
            sig = jax.nn.sigmoid(g)
            act = g * sig
            act_ref[:, cut] = act
            dact_ref[:, cut] = u * sig * (1.0 + g * (1.0 - sig))
            hid_ref[:, cut] = (act * u).astype(BF16)

    outs = [
        jax.ShapeDtypeStruct((m, hidden), F32),
        jax.ShapeDtypeStruct((m, hidden), F32),
        jax.ShapeDtypeStruct((m, hidden), BF16),
    ]
    args = (own, other, in_vmem(w_gate), in_vmem(w_up))
    return on_core(body, info, args, outs, "gate_up", 4 * m * model * hidden, limit(m), deps)


def hidden_grads(info, own, other, row0, act, dact, w_down, deps=()):
    hidden, model = w_down.shape
    m = own.shape[0]

    def body(s, refs, outs, _):
        own_ref, other_ref, act_ref, dact_ref, d_ref = refs
        ug_ref, gg_ref = outs
        rows = slice(row0, row0 + m)
        for at, to in cuts_of(hidden, HBLOCK):
            h = wide_dot(s, own_ref[...], other_ref[...], d_ref, slice(at, to))
            ug_ref[:, at:to] = (h * act_ref[rows, at:to]).astype(BF16)
            gg_ref[:, at:to] = (h * dact_ref[rows, at:to]).astype(BF16)

    outs = [jax.ShapeDtypeStruct((m, hidden), BF16)] * 2
    args = (own, other, act, dact, in_vmem(w_down))
    flops = 2 * m * model * hidden
    return on_core(body, info, args, outs, "hidden_grads", flops, LIMIT, deps)


def partial(info, up_grad, gate_grad, row0, m, w_gate, w_up, mine, deps=(), pieces=1):
    hidden, model = w_gate.shape
    half = model // 2
    each = m // pieces

    def body(s, refs, outs, _):
        ug_ref, gg_ref, g_ref, u_ref = refs
        rows = slice(row0, row0 + m)
        o = jnp.dot(gg_ref[rows], g_ref[:, side(s, half, mine)], preferred_element_type=F32)
        o = o + jnp.dot(ug_ref[rows], u_ref[:, side(s, half, mine)], preferred_element_type=F32)
        for i, out in enumerate(outs):
            out[...] = o[i * each : (i + 1) * each].astype(BF16)

    outs = [jax.ShapeDtypeStruct((each, half), BF16)] * pieces
    args = (up_grad, gate_grad, in_vmem(w_gate), in_vmem(w_up))
    return on_core(body, info, args, outs, "partial", 0, LIMIT, deps)


def down_grads(info, hid, gs, mine, filled=None, deps=(), db=512):
    m, hidden = hid.shape
    half = gs[0].shape[1]
    db = min(db, half)
    steps = half // db
    parts = [(i, 0, g.shape[0]) for i, g in enumerate(gs)]

    def column(k, s):
        return (0, k + (s[1] if mine else 1 - s[1]) * steps)

    def body(s, h_ref, *refs):
        o_ref, g_ref = refs[-2:]
        stack(g_ref, refs[: len(gs)], parts)
        o = lax.dot_general(h_ref[...], g_ref[...], TN, preferred_element_type=F32)
        o_ref[...] = o.astype(BF16)

    old = [] if filled is None else [in_hbm(filled)]
    return pl.pallas_call(
        body,
        grid_spec=pltpu.PrefetchScalarGridSpec(
            num_scalar_prefetch=1,
            grid=(steps,),
            in_specs=[pl.BlockSpec((m, hidden), lambda k, s: (0, 0))]
            + [pl.BlockSpec((g.shape[0], db), lambda k, s: (0, k)) for g in gs]
            + [pl.BlockSpec(memory_space=pltpu.HBM)] * len(old)
            + [pl.BlockSpec(memory_space=pl.ANY)] * len(deps),
            out_specs=pl.BlockSpec((hidden, db), column),
            scratch_shapes=[pltpu.VMEM((m, db), BF16)],
        ),
        out_shape=jax.ShapeDtypeStruct((hidden, 2 * half), BF16),
        input_output_aliases={2 + len(gs): 0} if old else {},
        compiler_params=pltpu.CompilerParams(vmem_limit_bytes=limit(m) * MIB),
        cost_estimate=cost(0, 1),
        name="down_grads",
    )(info, hid, *gs, *old, *deps)


def shards(tokens, token_grad_in, expert_ids, gate_weight, up_weight, down_weight):
    devices = lax.axis_size("expert")
    rows, model = tokens.shape
    half = model // 2
    share = devices // EXPERTS
    capacity = (rows + EXPERTS) // (EXPERTS + 1) + 1
    slots = -(-2 * capacity // 8) * 8
    bits = [b for b in range(1, share.bit_length() - 1)]
    index = lax.axis_index("expert")
    core = lax.rem(index, 2)
    info = jnp.stack([index // share, core]).astype(jnp.int32)

    def flip(x, bit):
        return lax.ppermute(x, "expert", [(i, i ^ (1 << bit)) for i in range(devices)])

    def plane_shift(x, d):
        return lax.ppermute(
            x, "expert", [(i, (i + d * share) % devices) for i in range(devices)]
        )

    def after(x, *others):
        return lax.optimization_barrier((x, *others))[0]

    def spread(parts):
        for bit in bits:
            parts = parts + [flip(p, bit) for p in parts]
        return parts

    def fold(halves, count, deps=(), far=()):
        for i, bit in enumerate(reversed(bits)):
            out, kept = halves
            got = flip(out, bit)
            if i + 1 < len(bits):
                halves = add_split(info, kept, [got], [(0, kept.shape[0])])
        return add_rounded(info, kept, got, count, deps, far)

    w_gate = jnp.swapaxes(gate_weight[0], 0, 1)
    w_up = jnp.swapaxes(up_weight[0], 0, 1)
    w_down = down_weight[0]

    mine, sent = halves(info, tokens, token_grad_in)
    received = flip(sent, 0)
    other_ids = flip(expert_ids, 0)
    near, tok, grad = pack(info, expert_ids, other_ids, mine, received, slots, capacity)

    t1, t3, t2 = plane_shift(tok[1], 1), plane_shift(tok[3], 3), plane_shift(tok[2], 2)
    near = spread([near])
    w_up = load(info, w_up, "load_up", (tok[1],))
    w_gate = load(info, w_gate, "load_gate", (tok[1], w_up))
    chips = len(near)
    n = chips * slots

    def by_plane(x, near_row, deps):
        rows = [(c, near_row, slots) for c in range(chips)]
        count = x[0].shape[0] // slots
        rows += [(chips + c, i * slots, slots) for i in range(count) for c in range(chips)]
        return join(info, [*near, *x], rows, deps)

    t = joined(info, [t1, t3, t2], (w_gate, w_up, *near))
    g1 = plane_shift(after(grad[1], t), 1)
    g3 = plane_shift(after(grad[3], t), 3)
    t = by_plane(spread([t]), 0, (g1, g3))
    t_other = flip(t, 0)
    g2 = plane_shift(after(grad[2], t), 2)
    g13 = spread([joined(info, [g1, g3], (t,))])
    act, dact, hid = gate_up(info, t, t_other, w_gate, w_up)

    g13 = by_plane(g13, slots, (hid, g2))
    g13_other = flip(g13, 0)
    g2 = spread([after(g2, g13)])
    up_grad, gate_grad = hidden_grads(info, g13, g13_other, 0, act, dact, w_down)
    g2 = joined(info, g2, (up_grad,))
    g2_other = flip(g2, 0)

    def back(row0, rows, mine, deps=()):
        return partial(info, up_grad, gate_grad, row0, rows, w_gate, w_up, mine, deps)[0]

    got = flip(back(n, 2 * n, False, (g2,)), 0)
    kept = back(n, 2 * n, True)
    rows13 = [(p * n + c * slots, slots) for c in range(chips) for p in range(2)]
    sum13 = add_split(info, kept, [got], rows13)

    up_grad2, gate_grad2 = hidden_grads(
        info, g2, g2_other, 3 * n, act, dact, w_down, (sum13[0],)
    )
    halves2 = (up_grad2, gate_grad2, 0, n, w_gate, w_up)
    got = [flip(x, 0) for x in partial(info, *halves2, False, (), chips)]
    kept = partial(info, *halves2, True)[0]
    far1, far3 = fold(sum13, 2)
    sum2 = add_split(info, kept, got, [(0, n)], (far1,))
    piece1, piece3 = plane_shift(far1, EXPERTS - 1), plane_shift(far3, EXPERTS - 3)

    got = flip(back(0, n, False, (sum2[0],)), 0)
    kept = back(0, n, True)
    (far2,) = fold(sum2, 1, (kept,))
    piece2 = plane_shift(far2, EXPERTS - 2)
    sum0 = add_split(info, kept, [got], [(0, n)])
    down_grad = down_grads(info, hid, [g13, g2], True, None, (far2, sum0[0]))
    down_grad = down_grads(info, hid, [g13_other, g2_other], False, down_grad, (piece1, piece3))
    (piece0,) = fold(sum0, 1)
    pieces = {0: piece0, 1: piece1, 2: piece2, 3: piece3}
    mine, theirs = unpack(
        info,
        expert_ids,
        other_ids,
        [pieces[d] for d in range(EXPERTS)],
        slots,
        capacity,
        (down_grad,),
    )
    got = flip(theirs, 0)
    input_grad = jnp.where(
        core == 0,
        jnp.concatenate([mine, got], axis=1),
        jnp.concatenate([got, mine], axis=1),
    )
    return (input_grad, down_grad[None])


def solution(mesh):
    placed = (
        P(("groups", "expert"), None),
        P(("groups", "expert"), None),
        P(("groups", "expert"), None),
        P("expert", None, None),
        P("expert", None, None),
        P("expert", None, None),
    )
    return jax.shard_map(
        shards,
        mesh=mesh,
        in_specs=placed,
        out_specs=(P(("groups", "expert"), None), P(("groups", "expert"), None, None)),
        check_vma=False,
    )
```

```python
import jax
import jax.numpy as jnp
from jax import lax
from jax.experimental import pallas as pl
from jax.experimental.pallas import tpu as pltpu
from jax.sharding import PartitionSpec as P

EXPERTS = 4
F32, BF16 = jnp.float32, jnp.bfloat16
NT = (((1,), (1,)), ((), ()))
TN = (((0,), (0,)), ((), ()))
MIB = 1024 * 1024
HBLOCK = 512
LIMIT = 12


def limit(rows):
    return LIMIT if rows <= 448 else 28


def cost(flops, nbytes):
    return pl.CostEstimate(flops=flops, bytes_accessed=nbytes, transcendentals=0)


def on_core(body, info, args, outs, name, flops, limit, deps=(), scratch=(), far=(), hbm=0):
    if hbm:
        args = (*args[:-hbm], *[in_hbm(x) for x in args[-hbm:]])
    n, d = len(args), len(deps) + len(far)

    def run(s, *refs):
        body(s, refs[:n], refs[n + d : n + d + len(outs)], refs[n + d + len(outs) :])

    vmem = pl.BlockSpec(memory_space=pltpu.VMEM)
    nbytes = sum(a.size * a.dtype.itemsize for a in args) if flops else 1
    return pl.pallas_call(
        run,
        in_specs=[pl.BlockSpec(memory_space=pltpu.SMEM)]
        + [vmem] * (n - hbm)
        + [pl.BlockSpec(memory_space=pltpu.HBM)] * hbm
        + [pl.BlockSpec(memory_space=pl.ANY)] * len(deps)
        + [pl.BlockSpec(memory_space=pltpu.HBM)] * len(far),
        out_specs=[vmem] * len(outs),
        out_shape=outs,
        scratch_shapes=scratch,
        compiler_params=pltpu.CompilerParams(vmem_limit_bytes=limit * MIB),
        cost_estimate=cost(flops, nbytes),
        name=name,
    )(info, *args, *deps, *[in_hbm(x) for x in far])


def slot_map(ids, plane, slots, which, capacity):
    rows = ids.shape[0]
    lane = lax.broadcasted_iota(jnp.int32, (rows, 128), 1)
    onehot = jnp.where(ids == lane, 1.0, 0.0)
    row_i = lax.broadcasted_iota(jnp.int32, (rows, rows), 0)
    col_i = lax.broadcasted_iota(jnp.int32, (rows, rows), 1)
    earlier = jnp.where(col_i < row_i, 1.0, 0.0).astype(BF16)
    before = jnp.dot(earlier, onehot.astype(BF16), preferred_element_type=F32)
    slot = jnp.sum(before * onehot, axis=1, keepdims=True).astype(jnp.int32)
    shift = ids - plane
    shift = jnp.where(shift < 0, shift + EXPERTS, shift)
    target = shift * slots + which * capacity + slot
    target = jnp.where(ids < EXPERTS, target, -1)
    place = lax.broadcasted_iota(jnp.int32, (rows, EXPERTS * slots), 1)
    return jnp.where(target == place, 1.0, 0.0).astype(BF16)


def side(s, half, mine):
    return pl.ds(pl.multiple_of((s[1] if mine else 1 - s[1]) * half, 128), half)


def halves(info, tokens, grads):
    rows, model = tokens.shape
    half = model // 2

    def body(s, refs, outs, scratch):
        copies = [
            pltpu.make_async_copy(
                ref.at[:, side(s, half, mine)],
                outs[0 if mine else 1].at[pl.ds(i * rows, rows)],
                scratch[0].at[2 * i + mine],
            )
            for i, ref in enumerate(refs)
            for mine in (False, True)
        ]
        for copy in copies:
            copy.start()
        for copy in copies:
            copy.wait()

    outs = [jax.ShapeDtypeStruct((2 * rows, half), BF16)] * 2
    scratch = [pltpu.SemaphoreType.DMA((4,))]
    return on_core(body, info, (tokens, grads), outs, "halves", 0, LIMIT, (), scratch, (), 2)


def pack(info, ids, other_ids, mine, received, slots, capacity):
    rows, half = mine.shape[0] // 2, mine.shape[1]

    def body(s, refs, outs, _):
        ids_ref, oids_ref, mine_ref, got_ref = refs
        p = slot_map(ids_ref[...], s[0], slots, s[1], capacity)
        q = slot_map(oids_ref[...], s[0], slots, 1 - s[1], capacity)
        for i in range(2):
            cut = slice(i * rows, (i + 1) * rows)
            got = lax.dot_general(p, mine_ref[cut], TN, preferred_element_type=F32)
            got = got + lax.dot_general(q, got_ref[cut], TN, preferred_element_type=F32)
            got = got.astype(BF16)
            for d in range(EXPERTS):
                outs[i * EXPERTS + d][...] = got[d * slots : (d + 1) * slots]

    outs = [jax.ShapeDtypeStruct((slots, half), BF16)] * (2 * EXPERTS)
    args = (ids, other_ids, mine, received)
    made = on_core(body, info, args, outs, "pack", 8 * rows * 4 * slots * half, LIMIT)
    return made[:EXPERTS], made[EXPERTS:]


def unpack(info, ids, other_ids, pieces, slots, capacity, deps):
    rows, width = ids.shape[0], pieces[0].shape[1]

    def body(s, refs, outs, _):
        p = slot_map(refs[0][...], s[0], slots, s[1], capacity)
        q = slot_map(refs[1][...], s[0], slots, 1 - s[1], capacity)
        z = jnp.concatenate([r[...].astype(F32) for r in refs[2:]], axis=0).astype(BF16)
        outs[0][...] = jnp.dot(p, z, preferred_element_type=F32).astype(BF16)
        outs[1][...] = jnp.dot(q, z, preferred_element_type=F32).astype(BF16)

    outs = [jax.ShapeDtypeStruct((rows, width), BF16)] * 2
    args = (ids, other_ids, *pieces)
    flops = 4 * rows * EXPERTS * slots * width
    return on_core(body, info, args, outs, "unpack", flops, LIMIT, (), (), deps)


def stack(to, refs, parts):
    at = 0
    for which, row, rows in parts:
        to[at : at + rows] = refs[which][row : row + rows]
        at += rows


def join(info, arrays, parts, deps=()):
    def body(s, refs, outs, _):
        stack(outs[0], refs, parts)

    rows, width = sum(p[2] for p in parts), arrays[0].shape[1]
    outs = [jax.ShapeDtypeStruct((rows, width), arrays[0].dtype)]
    return on_core(body, info, arrays, outs, "join", 0, LIMIT, deps)[0]


def joined(info, arrays, deps=()):
    return join(info, arrays, [(i, 0, a.shape[0]) for i, a in enumerate(arrays)], deps)


def add_split(info, a, b, parts, deps=()):
    rows, width = sum(p[1] for p in parts), a.shape[1]
    mid, size = rows // 2, b[0].shape[0]
    each = min(mid, size, min(p[1] for p in parts))
    pieces = [row + i for row, n in parts for i in range(0, n, each)]

    def body(s, refs, outs, _):
        for i, row in enumerate(pieces):
            at, y = i * each, refs[1 + row // size]
            total = refs[0][row : row + each].astype(F32)
            total = total + y[row % size : row % size + each].astype(F32)
            if at < mid:
                outs[1][at : at + each] = total
            else:
                outs[0][at - mid : at - mid + each] = total.astype(BF16)

    outs = [
        jax.ShapeDtypeStruct((rows - mid, width), BF16),
        jax.ShapeDtypeStruct((mid, width), F32),
    ]
    return on_core(body, info, (a, *b), outs, "add_split", 0, LIMIT, deps)


def add_rounded(info, a, b, count, deps=(), far=()):
    each = a.shape[0] // count

    def body(s, refs, outs, _):
        for i, out in enumerate(outs):
            cut = slice(i * each, (i + 1) * each)
            out[...] = (refs[0][cut].astype(F32) + refs[1][cut].astype(F32)).astype(BF16)

    outs = [jax.ShapeDtypeStruct((each, a.shape[1]), BF16)] * count
    return on_core(body, info, (a, b), outs, "add_rounded", 0, LIMIT, deps, (), far)


def in_vmem(x):
    return pltpu.with_memory_space_constraint(x, pltpu.VMEM)


def in_hbm(x):
    return pltpu.with_memory_space_constraint(x, pltpu.HBM)


def load(info, w, name, deps=()):
    def body(s, w_ref, *rest):
        out_ref, sem = rest[-2:]
        copy = pltpu.make_async_copy(w_ref, out_ref, sem)
        copy.start()
        copy.wait()

    return pl.pallas_call(
        body,
        in_specs=[pl.BlockSpec(memory_space=pltpu.SMEM)]
        + [pl.BlockSpec(memory_space=pltpu.HBM)]
        + [pl.BlockSpec(memory_space=pl.ANY)] * len(deps),
        out_specs=pl.BlockSpec(memory_space=pltpu.VMEM),
        out_shape=pltpu.VMEM(w.shape, w.dtype),
        scratch_shapes=[pltpu.SemaphoreType.DMA],
        compiler_params=pltpu.CompilerParams(vmem_limit_bytes=LIMIT * MIB),
        cost_estimate=cost(0, 2 * w.size * 2),
        name=name,
    )(info, in_hbm(w), *deps)


def cuts_of(size, step):
    return [(at, min(at + step, size)) for at in range(0, size, step)]


def wide_dot(s, own, other, w_ref, cut):
    half = own.shape[1]
    return lax.dot_general(
        own, w_ref[cut, side(s, half, True)], NT, preferred_element_type=F32
    ) + lax.dot_general(other, w_ref[cut, side(s, half, False)], NT, preferred_element_type=F32)


def gate_up(info, own, other, w_gate, w_up, deps=()):
    hidden, model = w_gate.shape
    m = own.shape[0]

    def body(s, refs, outs, _):
        own_ref, other_ref, g_ref, u_ref = refs
        act_ref, dact_ref, hid_ref = outs
        for at, to in cuts_of(hidden, HBLOCK):
            cut = slice(at, to)
            g = wide_dot(s, own_ref[...], other_ref[...], g_ref, cut)
            u = wide_dot(s, own_ref[...], other_ref[...], u_ref, cut)
            sig = jax.nn.sigmoid(g)
            act = g * sig
            act_ref[:, cut] = act.astype(BF16)
            dact_ref[:, cut] = (u * sig * (1.0 + g * (1.0 - sig))).astype(BF16)
            hid_ref[:, cut] = (act * u).astype(BF16)

    outs = [
        jax.ShapeDtypeStruct((m, hidden), BF16),
        jax.ShapeDtypeStruct((m, hidden), BF16),
        jax.ShapeDtypeStruct((m, hidden), BF16),
    ]
    args = (own, other, in_vmem(w_gate), in_vmem(w_up))
    return on_core(body, info, args, outs, "gate_up", 4 * m * model * hidden, limit(m), deps)


def hidden_grads(info, own, other, row0, act, dact, w_down, deps=(), stream=False):
    hidden, model = w_down.shape
    m = own.shape[0]

    def body(s, refs, outs, scratch):
        own_ref, other_ref, act_ref, dact_ref, d_ref = refs
        ug_ref, gg_ref = outs
        rows = slice(row0, row0 + m)
        cuts, copies = cuts_of(hidden, HBLOCK), []
        if stream:
            ring, sem = scratch
            copies = [
                pltpu.make_async_copy(
                    d_ref.at[pl.ds(at, to - at)], ring.at[j % 2, pl.ds(0, to - at)], sem.at[j]
                )
                for j, (at, to) in enumerate(cuts)
            ]
            for copy in copies[:2]:
                copy.start()
        for j, (at, to) in enumerate(cuts):
            if stream:
                copies[j].wait()
                block, cut = ring.at[j % 2], slice(0, to - at)
            else:
                block, cut = d_ref, slice(at, to)
            h = wide_dot(s, own_ref[...], other_ref[...], block, cut)
            if j + 2 < len(copies):
                copies[j + 2].start()
            ug_ref[:, at:to] = (h * act_ref[rows, at:to]).astype(BF16)
            gg_ref[:, at:to] = (h * dact_ref[rows, at:to]).astype(BF16)

    outs = [jax.ShapeDtypeStruct((m, hidden), BF16)] * 2
    if stream:
        scratch = [
            pltpu.VMEM((2, HBLOCK, model), BF16),
            pltpu.SemaphoreType.DMA((pl.cdiv(hidden, HBLOCK),)),
        ]
        args = (own, other, act, dact, w_down)
        return on_core(body, info, args, outs, "hidden_grads", 0, limit(m), deps, scratch, (), 1)
    args = (own, other, act, dact, in_vmem(w_down))
    return on_core(body, info, args, outs, "hidden_grads", 0, LIMIT, deps)


def partial(info, up_grad, gate_grad, row0, m, w_gate, w_up, mine, deps=(), pieces=1):
    hidden, model = w_gate.shape
    half = model // 2
    each = m // pieces

    def body(s, refs, outs, _):
        ug_ref, gg_ref, g_ref, u_ref = refs
        rows = slice(row0, row0 + m)
        o = jnp.dot(gg_ref[rows], g_ref[:, side(s, half, mine)], preferred_element_type=F32)
        o = o + jnp.dot(ug_ref[rows], u_ref[:, side(s, half, mine)], preferred_element_type=F32)
        for i, out in enumerate(outs):
            out[...] = o[i * each : (i + 1) * each].astype(BF16)

    outs = [jax.ShapeDtypeStruct((each, half), BF16)] * pieces
    args = (up_grad, gate_grad, in_vmem(w_gate), in_vmem(w_up))
    return on_core(body, info, args, outs, "partial", 0, LIMIT, deps)


def down_grads(info, hids, gs, mine, filled=None, deps=(), turns=(0, 1), db=512):
    m, hidden = sum(h.shape[0] for h in hids), hids[0].shape[1]
    half = gs[0].shape[1]
    steps = half // db
    count = steps // turns[1]
    first = turns[0] * count
    parts = [(i, 0, g.shape[0]) for i, g in enumerate(gs)]

    def column(k, s):
        return (0, first + k + (s[1] if mine else 1 - s[1]) * steps)

    hid_parts = [(i, 0, h.shape[0]) for i, h in enumerate(hids)]

    def body(s, *refs):
        o_ref, g_ref, h_ref = refs[-3:]

        @pl.when(pl.program_id(0) == 0)
        def _():
            stack(h_ref, refs[: len(hids)], hid_parts)

        stack(g_ref, refs[len(hids) : len(hids) + len(gs)], parts)
        o = lax.dot_general(h_ref[...], g_ref[...], TN, preferred_element_type=F32)
        o_ref[...] = o.astype(BF16)

    old = [] if filled is None else [in_hbm(filled)]
    return pl.pallas_call(
        body,
        grid_spec=pltpu.PrefetchScalarGridSpec(
            num_scalar_prefetch=1,
            grid=(count,),
            in_specs=[pl.BlockSpec(h.shape, lambda k, s: (0, 0)) for h in hids]
            + [pl.BlockSpec((g.shape[0], db), lambda k, s: (0, first + k)) for g in gs]
            + [pl.BlockSpec(memory_space=pltpu.HBM)] * len(old)
            + [pl.BlockSpec(memory_space=pl.ANY)] * len(deps),
            out_specs=pl.BlockSpec((hidden, db), column),
            scratch_shapes=[pltpu.VMEM((m, db), BF16), pltpu.VMEM((m, hidden), BF16)],
        ),
        out_shape=jax.ShapeDtypeStruct((hidden, 2 * half), BF16),
        input_output_aliases={1 + len(hids) + len(gs): 0} if old else {},
        compiler_params=pltpu.CompilerParams(vmem_limit_bytes=limit(m) * MIB),
        cost_estimate=cost(0, 1),
        name="down_grads",
    )(info, *hids, *gs, *old, *deps)


def shards(tokens, token_grad_in, expert_ids, gate_weight, up_weight, down_weight):
    devices = lax.axis_size("expert")
    rows, model = tokens.shape
    half = model // 2
    share = devices // EXPERTS
    capacity = (rows + EXPERTS) // (EXPERTS + 1) + 1
    slots = -(-2 * capacity // 8) * 8
    bits = [b for b in range(1, share.bit_length() - 1)]
    index = lax.axis_index("expert")
    core = lax.rem(index, 2)
    info = jnp.stack([index // share, core]).astype(jnp.int32)

    def flip(x, bit):
        return lax.ppermute(x, "expert", [(i, i ^ (1 << bit)) for i in range(devices)])

    def plane_shift(x, d):
        return lax.ppermute(
            x, "expert", [(i, (i + d * share) % devices) for i in range(devices)]
        )

    def after(x, *others):
        return lax.optimization_barrier((x, *others))[0]

    def spread(parts):
        for bit in bits:
            parts = parts + [flip(p, bit) for p in parts]
        return parts

    def fold(halves, count, deps=(), far=()):
        for i, bit in enumerate(reversed(bits)):
            out, kept = halves
            got = flip(out, bit)
            if i + 1 < len(bits):
                halves = add_split(info, kept, [got], [(0, kept.shape[0])])
        return add_rounded(info, kept, got, count, deps, far)

    w_gate = jnp.swapaxes(gate_weight[0], 0, 1)
    w_up = jnp.swapaxes(up_weight[0], 0, 1)
    w_down = down_weight[0]

    mine, sent = halves(info, tokens, token_grad_in)
    received = flip(sent, 0)
    other_ids = flip(expert_ids, 0)
    tok, grad = pack(info, expert_ids, other_ids, mine, received, slots, capacity)

    t1, t3, t2 = plane_shift(tok[1], 1), plane_shift(tok[3], 3), plane_shift(tok[2], 2)
    near_tok, near_grad = spread([tok[0]]), spread([grad[0]])
    w_up = load(info, w_up, "load_up", (tok[1],))
    w_gate = load(info, w_gate, "load_gate", (tok[1], w_up))
    chips = len(near_tok)
    n = chips * slots

    def by_plane(x, deps):
        count = x[0].shape[0] // slots
        rows = [(c, i * slots, slots) for i in range(count) for c in range(chips)]
        return join(info, x, rows, deps)

    def back(grads, row0, rows, mine, deps=(), pieces=1):
        return partial(info, *grads, row0, rows, w_gate, w_up, mine, deps, pieces)

    t = joined(info, [t1, t3, t2], (w_gate, w_up, *near_tok, *near_grad))
    g1 = plane_shift(after(grad[1], t), 1)
    g3 = plane_shift(after(grad[3], t), 3)
    t = spread([t])

    near_t, near_g = joined(info, near_tok), joined(info, near_grad)
    near_t_other, near_g_other = flip(near_t, 0), flip(near_g, 0)
    act0, dact0, hid0 = gate_up(info, near_t, near_t_other, w_gate, w_up)
    grads0 = hidden_grads(info, near_g, near_g_other, 0, act0, dact0, w_down)

    t = by_plane(t, (g1, g3, grads0[0]))
    t_other = flip(t, 0)
    g13 = joined(info, [g1, g3], (t,))
    g2 = plane_shift(after(grad[2], g13), 2)
    kept0 = back(grads0, 0, n, True, (g13,))[0]
    g13 = spread([g13])
    act, dact, hid = gate_up(info, t, t_other, w_gate, w_up, (kept0,))

    g13 = by_plane(g13, (hid, g2))
    g13_other = flip(g13, 0)
    g2 = spread([after(g2, g13)])
    sent0 = back(grads0, 0, n, False, (g13,))[0]
    got0 = flip(sent0, 0)
    grads13 = hidden_grads(info, g13, g13_other, 0, act, dact, w_down, (sent0,))
    g2 = joined(info, g2, (grads13[0],))
    g2_other = flip(g2, 0)
    got = flip(back(grads13, 0, 2 * n, False, (g2,))[0], 0)
    kept = back(grads13, 0, 2 * n, True)[0]
    rows13 = [(p * n + c * slots, slots) for c in range(chips) for p in range(2)]
    sum13 = add_split(info, kept, [got], rows13)
    sum0 = add_split(info, kept0, [got0], [(0, n)], (sum13[0],))
    grads2 = hidden_grads(
        info, g2, g2_other, 2 * n, act, dact, w_down, (sum13[0],), True
    )
    got = [flip(x, 0) for x in back(grads2, 0, n, False, (), chips)]
    kept = back(grads2, 0, n, True)[0]
    far1, far3 = fold(sum13, 2)
    sum2 = add_split(info, kept, got, [(0, n)], (far1,))
    piece1, piece3 = plane_shift(far1, EXPERTS - 1), plane_shift(far3, EXPERTS - 3)

    hids, gs = [hid0, hid], [near_g, g13, g2]
    down_grad = down_grads(info, hids, gs, True, None, (sum2[0], far1))
    (far2,) = fold(sum2, 1, (), (down_grad,))
    piece2 = plane_shift(far2, EXPERTS - 2)
    gs = [near_g_other, g13_other, g2_other]
    down_grad = down_grads(info, hids, gs, False, down_grad, (far2, piece1, piece3))
    (piece0,) = fold(sum0, 1, (), (down_grad,))
    pieces = {0: piece0, 1: piece1, 2: piece2, 3: piece3}
    mine, theirs = unpack(
        info,
        expert_ids,
        other_ids,
        [pieces[d] for d in range(EXPERTS)],
        slots,
        capacity,
        (down_grad,),
    )
    got = flip(theirs, 0)
    input_grad = jnp.where(
        core == 0,
        jnp.concatenate([mine, got], axis=1),
        jnp.concatenate([got, mine], axis=1),
    )
    return (input_grad, down_grad[None])


def solution(mesh):
    placed = (
        P(("groups", "expert"), None),
        P(("groups", "expert"), None),
        P(("groups", "expert"), None),
        P("expert", None, None),
        P("expert", None, None),
        P("expert", None, None),
    )
    return jax.shard_map(
        shards,
        mesh=mesh,
        in_specs=placed,
        out_specs=(P(("groups", "expert"), None), P(("groups", "expert"), None, None)),
        check_vma=False,
    )
```

```python
import jax
import jax.numpy as jnp
from jax import lax
from jax.experimental import pallas as pl
from jax.experimental.pallas import tpu as pltpu
from jax.sharding import PartitionSpec as P

EXPERTS = 4
F32, BF16 = jnp.float32, jnp.bfloat16
NT = (((1,), (1,)), ((), ()))
TN = (((0,), (0,)), ((), ()))
MIB = 1024 * 1024
HBLOCK = 512
LIMIT = 12


def limit(rows):
    return LIMIT if rows <= 448 else 28


def cost(flops, nbytes):
    return pl.CostEstimate(flops=flops, bytes_accessed=nbytes, transcendentals=0)


def on_core(body, info, args, outs, name, flops, limit, deps=(), scratch=(), far=(), hbm=0):
    if hbm:
        args = (*args[:-hbm], *[in_hbm(x) for x in args[-hbm:]])
    n, d = len(args), len(deps) + len(far)

    def run(s, *refs):
        body(s, refs[:n], refs[n + d : n + d + len(outs)], refs[n + d + len(outs) :])

    vmem = pl.BlockSpec(memory_space=pltpu.VMEM)
    nbytes = sum(a.size * a.dtype.itemsize for a in args) if flops else 1
    return pl.pallas_call(
        run,
        in_specs=[pl.BlockSpec(memory_space=pltpu.SMEM)]
        + [vmem] * (n - hbm)
        + [pl.BlockSpec(memory_space=pltpu.HBM)] * hbm
        + [pl.BlockSpec(memory_space=pl.ANY)] * len(deps)
        + [pl.BlockSpec(memory_space=pltpu.HBM)] * len(far),
        out_specs=[vmem] * len(outs),
        out_shape=outs,
        scratch_shapes=scratch,
        compiler_params=pltpu.CompilerParams(vmem_limit_bytes=limit * MIB),
        cost_estimate=cost(flops, nbytes),
        name=name,
    )(info, *args, *deps, *[in_hbm(x) for x in far])


def slot_map(ids, plane, slots, which, capacity):
    rows = ids.shape[0]
    lane = lax.broadcasted_iota(jnp.int32, (rows, 128), 1)
    onehot = jnp.where(ids == lane, 1.0, 0.0)
    row_i = lax.broadcasted_iota(jnp.int32, (rows, rows), 0)
    col_i = lax.broadcasted_iota(jnp.int32, (rows, rows), 1)
    earlier = jnp.where(col_i < row_i, 1.0, 0.0).astype(BF16)
    before = jnp.dot(earlier, onehot.astype(BF16), preferred_element_type=F32)
    slot = jnp.sum(before * onehot, axis=1, keepdims=True).astype(jnp.int32)
    shift = ids - plane
    shift = jnp.where(shift < 0, shift + EXPERTS, shift)
    target = shift * slots + which * capacity + slot
    target = jnp.where(ids < EXPERTS, target, -1)
    place = lax.broadcasted_iota(jnp.int32, (rows, EXPERTS * slots), 1)
    return jnp.where(target == place, 1.0, 0.0).astype(BF16)


def side(s, half, mine):
    return pl.ds(pl.multiple_of((s[1] if mine else 1 - s[1]) * half, 128), half)


def halves(info, tokens, grads):
    rows, model = tokens.shape
    half = model // 2

    def body(s, refs, outs, scratch):
        copies = [
            pltpu.make_async_copy(
                ref.at[:, side(s, half, mine)],
                outs[0 if mine else 1].at[pl.ds(i * rows, rows)],
                scratch[0].at[2 * i + mine],
            )
            for i, ref in enumerate(refs)
            for mine in (False, True)
        ]
        for copy in copies:
            copy.start()
        for copy in copies:
            copy.wait()

    outs = [jax.ShapeDtypeStruct((2 * rows, half), BF16)] * 2
    scratch = [pltpu.SemaphoreType.DMA((4,))]
    return on_core(body, info, (tokens, grads), outs, "halves", 0, LIMIT, (), scratch, (), 2)


def pack(info, ids, other_ids, mine, received, slots, capacity):
    rows, half = mine.shape[0] // 2, mine.shape[1]

    def body(s, refs, outs, _):
        ids_ref, oids_ref, mine_ref, got_ref = refs
        p = slot_map(ids_ref[...], s[0], slots, s[1], capacity)
        q = slot_map(oids_ref[...], s[0], slots, 1 - s[1], capacity)
        for i in range(2):
            cut = slice(i * rows, (i + 1) * rows)
            got = lax.dot_general(p, mine_ref[cut], TN, preferred_element_type=F32)
            got = got + lax.dot_general(q, got_ref[cut], TN, preferred_element_type=F32)
            got = got.astype(BF16)
            for d in range(EXPERTS):
                outs[i * EXPERTS + d][...] = got[d * slots : (d + 1) * slots]

    outs = [jax.ShapeDtypeStruct((slots, half), BF16)] * (2 * EXPERTS)
    args = (ids, other_ids, mine, received)
    made = on_core(body, info, args, outs, "pack", 8 * rows * 4 * slots * half, LIMIT)
    return made[:EXPERTS], made[EXPERTS:]


def unpack(info, ids, other_ids, pieces, slots, capacity, deps):
    rows, width = ids.shape[0], pieces[0].shape[1]

    def body(s, refs, outs, _):
        p = slot_map(refs[0][...], s[0], slots, s[1], capacity)
        q = slot_map(refs[1][...], s[0], slots, 1 - s[1], capacity)
        z = jnp.concatenate([r[...].astype(F32) for r in refs[2:]], axis=0).astype(BF16)
        outs[0][...] = jnp.dot(p, z, preferred_element_type=F32).astype(BF16)
        outs[1][...] = jnp.dot(q, z, preferred_element_type=F32).astype(BF16)

    outs = [jax.ShapeDtypeStruct((rows, width), BF16)] * 2
    args = (ids, other_ids, *pieces)
    flops = 4 * rows * EXPERTS * slots * width
    return on_core(body, info, args, outs, "unpack", flops, LIMIT, (), (), deps)


def stack(to, refs, parts):
    at = 0
    for which, row, rows in parts:
        to[at : at + rows] = refs[which][row : row + rows]
        at += rows


def join(info, arrays, parts, deps=()):
    def body(s, refs, outs, _):
        stack(outs[0], refs, parts)

    rows, width = sum(p[2] for p in parts), arrays[0].shape[1]
    outs = [jax.ShapeDtypeStruct((rows, width), arrays[0].dtype)]
    return on_core(body, info, arrays, outs, "join", 0, LIMIT, deps)[0]


def joined(info, arrays, deps=()):
    return join(info, arrays, [(i, 0, a.shape[0]) for i, a in enumerate(arrays)], deps)


def add_split(info, a, b, parts, deps=()):
    rows, width = sum(p[1] for p in parts), a.shape[1]
    mid, size = rows // 2, b[0].shape[0]
    each = min(mid, size, min(p[1] for p in parts))
    pieces = [row + i for row, n in parts for i in range(0, n, each)]

    def body(s, refs, outs, _):
        for i, row in enumerate(pieces):
            at, y = i * each, refs[1 + row // size]
            total = refs[0][row : row + each].astype(F32)
            total = total + y[row % size : row % size + each].astype(F32)
            if at < mid:
                outs[1][at : at + each] = total
            else:
                outs[0][at - mid : at - mid + each] = total.astype(BF16)

    outs = [
        jax.ShapeDtypeStruct((rows - mid, width), BF16),
        jax.ShapeDtypeStruct((mid, width), F32),
    ]
    return on_core(body, info, (a, *b), outs, "add_split", 0, LIMIT, deps)


def add_rounded(info, a, b, count, deps=(), far=()):
    each = a.shape[0] // count

    def body(s, refs, outs, _):
        for i, out in enumerate(outs):
            cut = slice(i * each, (i + 1) * each)
            out[...] = (refs[0][cut].astype(F32) + refs[1][cut].astype(F32)).astype(BF16)

    outs = [jax.ShapeDtypeStruct((each, a.shape[1]), BF16)] * count
    return on_core(body, info, (a, b), outs, "add_rounded", 0, LIMIT, deps, (), far)


def in_vmem(x):
    return pltpu.with_memory_space_constraint(x, pltpu.VMEM)


def in_hbm(x):
    return pltpu.with_memory_space_constraint(x, pltpu.HBM)


def load(info, w, name, deps=()):
    def body(s, w_ref, *rest):
        out_ref, sem = rest[-2:]
        copy = pltpu.make_async_copy(w_ref, out_ref, sem)
        copy.start()
        copy.wait()

    return pl.pallas_call(
        body,
        in_specs=[pl.BlockSpec(memory_space=pltpu.SMEM)]
        + [pl.BlockSpec(memory_space=pltpu.HBM)]
        + [pl.BlockSpec(memory_space=pl.ANY)] * len(deps),
        out_specs=pl.BlockSpec(memory_space=pltpu.VMEM),
        out_shape=pltpu.VMEM(w.shape, w.dtype),
        scratch_shapes=[pltpu.SemaphoreType.DMA],
        compiler_params=pltpu.CompilerParams(vmem_limit_bytes=LIMIT * MIB),
        cost_estimate=cost(0, 2 * w.size * 2),
        name=name,
    )(info, in_hbm(w), *deps)


def cuts_of(size, step):
    return [(at, min(at + step, size)) for at in range(0, size, step)]


def wide_dot(s, own, other, w_ref, cut):
    half = own.shape[1]
    return lax.dot_general(
        own, w_ref[cut, side(s, half, True)], NT, preferred_element_type=F32
    ) + lax.dot_general(other, w_ref[cut, side(s, half, False)], NT, preferred_element_type=F32)


def gate_up(info, own, other, w_gate, w_up, deps=()):
    hidden, model = w_gate.shape
    m = own.shape[0]

    def body(s, refs, outs, _):
        own_ref, other_ref, g_ref, u_ref = refs
        act_ref, dact_ref, hid_ref = outs
        for at, to in cuts_of(hidden, HBLOCK):
            cut = slice(at, to)
            g = wide_dot(s, own_ref[...], other_ref[...], g_ref, cut)
            u = wide_dot(s, own_ref[...], other_ref[...], u_ref, cut)
            sig = jax.nn.sigmoid(g)
            act = g * sig
            act_ref[:, cut] = act.astype(BF16)
            dact_ref[:, cut] = (u * sig * (1.0 + g * (1.0 - sig))).astype(BF16)
            hid_ref[:, cut] = (act * u).astype(BF16)

    outs = [
        jax.ShapeDtypeStruct((m, hidden), BF16),
        jax.ShapeDtypeStruct((m, hidden), BF16),
        jax.ShapeDtypeStruct((m, hidden), BF16),
    ]
    args = (own, other, in_vmem(w_gate), in_vmem(w_up))
    return on_core(body, info, args, outs, "gate_up", 4 * m * model * hidden, limit(m), deps)


def hidden_grads(info, own, other, row0, act, dact, w_down, deps=(), stream=False):
    hidden, model = w_down.shape
    m = own.shape[0]

    def body(s, refs, outs, scratch):
        own_ref, other_ref, act_ref, dact_ref, d_ref = refs
        ug_ref, gg_ref = outs
        rows = slice(row0, row0 + m)
        cuts, copies = cuts_of(hidden, HBLOCK), []
        if stream:
            ring, sem = scratch
            copies = [
                pltpu.make_async_copy(
                    d_ref.at[pl.ds(at, to - at)], ring.at[j % 2, pl.ds(0, to - at)], sem.at[j]
                )
                for j, (at, to) in enumerate(cuts)
            ]
            for copy in copies[:2]:
                copy.start()
        for j, (at, to) in enumerate(cuts):
            if stream:
                copies[j].wait()
                block, cut = ring.at[j % 2], slice(0, to - at)
            else:
                block, cut = d_ref, slice(at, to)
            h = wide_dot(s, own_ref[...], other_ref[...], block, cut)
            if j + 2 < len(copies):
                copies[j + 2].start()
            ug_ref[:, at:to] = (h * act_ref[rows, at:to]).astype(BF16)
            gg_ref[:, at:to] = (h * dact_ref[rows, at:to]).astype(BF16)

    outs = [jax.ShapeDtypeStruct((m, hidden), BF16)] * 2
    if stream:
        scratch = [
            pltpu.VMEM((2, HBLOCK, model), BF16),
            pltpu.SemaphoreType.DMA((pl.cdiv(hidden, HBLOCK),)),
        ]
        args = (own, other, act, dact, w_down)
        return on_core(body, info, args, outs, "hidden_grads", 0, limit(m), deps, scratch, (), 1)
    args = (own, other, act, dact, in_vmem(w_down))
    return on_core(body, info, args, outs, "hidden_grads", 0, LIMIT, deps)


def partial(info, up_grad, gate_grad, row0, m, w_gate, w_up, mine, deps=(), pieces=1):
    hidden, model = w_gate.shape
    half = model // 2
    each = m // pieces

    def body(s, refs, outs, _):
        ug_ref, gg_ref, g_ref, u_ref = refs
        rows = slice(row0, row0 + m)
        o = jnp.dot(gg_ref[rows], g_ref[:, side(s, half, mine)], preferred_element_type=F32)
        o = o + jnp.dot(ug_ref[rows], u_ref[:, side(s, half, mine)], preferred_element_type=F32)
        for i, out in enumerate(outs):
            out[...] = o[i * each : (i + 1) * each].astype(BF16)

    outs = [jax.ShapeDtypeStruct((each, half), BF16)] * pieces
    args = (up_grad, gate_grad, in_vmem(w_gate), in_vmem(w_up))
    return on_core(body, info, args, outs, "partial", 0, LIMIT, deps)


def down_grads(info, hids, gs, mine, filled=None, deps=(), turns=(0, 1), db=1024):
    m, hidden = sum(h.shape[0] for h in hids), hids[0].shape[1]
    half = gs[0].shape[1]
    steps = half // db
    count = steps // turns[1]
    first = turns[0] * count
    parts = [(i, 0, g.shape[0]) for i, g in enumerate(gs)]

    def column(k, s):
        return (0, first + k + (s[1] if mine else 1 - s[1]) * steps)

    hid_parts = [(i, 0, h.shape[0]) for i, h in enumerate(hids)]

    def body(s, *refs):
        o_ref, g_ref, h_ref = refs[-3:]

        @pl.when(pl.program_id(0) == 0)
        def _():
            stack(h_ref, refs[: len(hids)], hid_parts)

        stack(g_ref, refs[len(hids) : len(hids) + len(gs)], parts)
        o = lax.dot_general(h_ref[...], g_ref[...], TN, preferred_element_type=F32)
        o_ref[...] = o.astype(BF16)

    old = [] if filled is None else [in_hbm(filled)]
    return pl.pallas_call(
        body,
        grid_spec=pltpu.PrefetchScalarGridSpec(
            num_scalar_prefetch=1,
            grid=(count,),
            in_specs=[pl.BlockSpec(h.shape, lambda k, s: (0, 0)) for h in hids]
            + [pl.BlockSpec((g.shape[0], db), lambda k, s: (0, first + k)) for g in gs]
            + [pl.BlockSpec(memory_space=pltpu.HBM)] * len(old)
            + [pl.BlockSpec(memory_space=pl.ANY)] * len(deps),
            out_specs=pl.BlockSpec((hidden, db), column),
            scratch_shapes=[pltpu.VMEM((m, db), BF16), pltpu.VMEM((m, hidden), BF16)],
        ),
        out_shape=jax.ShapeDtypeStruct((hidden, 2 * half), BF16),
        input_output_aliases={1 + len(hids) + len(gs): 0} if old else {},
        compiler_params=pltpu.CompilerParams(vmem_limit_bytes=(limit(m) + 12) * MIB),
        cost_estimate=cost(0, 1),
        name="down_grads",
    )(info, *hids, *gs, *old, *deps)


def shards(tokens, token_grad_in, expert_ids, gate_weight, up_weight, down_weight):
    devices = lax.axis_size("expert")
    rows, model = tokens.shape
    half = model // 2
    share = devices // EXPERTS
    capacity = (rows + EXPERTS) // (EXPERTS + 1) + 1
    slots = -(-2 * capacity // 8) * 8
    bits = [b for b in range(1, share.bit_length() - 1)]
    index = lax.axis_index("expert")
    core = lax.rem(index, 2)
    info = jnp.stack([index // share, core]).astype(jnp.int32)

    def flip(x, bit):
        return lax.ppermute(x, "expert", [(i, i ^ (1 << bit)) for i in range(devices)])

    def plane_shift(x, d):
        return lax.ppermute(
            x, "expert", [(i, (i + d * share) % devices) for i in range(devices)]
        )

    def after(x, *others):
        return lax.optimization_barrier((x, *others))[0]

    def spread(parts):
        for bit in bits:
            parts = parts + [flip(p, bit) for p in parts]
        return parts

    def fold(halves, count, deps=(), far=()):
        for i, bit in enumerate(reversed(bits)):
            out, kept = halves
            got = flip(out, bit)
            if i + 1 < len(bits):
                halves = add_split(info, kept, [got], [(0, kept.shape[0])])
        return add_rounded(info, kept, got, count, deps, far)

    w_gate = jnp.swapaxes(gate_weight[0], 0, 1)
    w_up = jnp.swapaxes(up_weight[0], 0, 1)
    w_down = down_weight[0]

    mine, sent = halves(info, tokens, token_grad_in)
    received = flip(sent, 0)
    other_ids = flip(expert_ids, 0)
    tok, grad = pack(info, expert_ids, other_ids, mine, received, slots, capacity)

    t1, t3, t2 = plane_shift(tok[1], 1), plane_shift(tok[3], 3), plane_shift(tok[2], 2)
    near_tok, near_grad = spread([tok[0]]), spread([grad[0]])
    w_up = load(info, w_up, "load_up", (tok[1],))
    w_gate = load(info, w_gate, "load_gate", (tok[1], w_up))
    chips = len(near_tok)
    n = chips * slots

    def by_plane(x, deps):
        count = x[0].shape[0] // slots
        rows = [(c, i * slots, slots) for i in range(count) for c in range(chips)]
        return join(info, x, rows, deps)

    def back(grads, row0, rows, mine, deps=(), pieces=1):
        return partial(info, *grads, row0, rows, w_gate, w_up, mine, deps, pieces)

    t = joined(info, [t1, t3, t2], (w_gate, w_up, *near_tok, *near_grad))
    g1 = plane_shift(after(grad[1], t), 1)
    g3 = plane_shift(after(grad[3], t), 3)
    t = spread([t])

    near_t, near_g = joined(info, near_tok), joined(info, near_grad)
    near_t_other, near_g_other = flip(near_t, 0), flip(near_g, 0)
    act0, dact0, hid0 = gate_up(info, near_t, near_t_other, w_gate, w_up)
    grads0 = hidden_grads(info, near_g, near_g_other, 0, act0, dact0, w_down)

    t = by_plane(t, (g1, g3, grads0[0]))
    t_other = flip(t, 0)
    g13 = joined(info, [g1, g3], (t,))
    g2 = plane_shift(after(grad[2], g13), 2)
    kept0 = back(grads0, 0, n, True, (g13,))[0]
    g13 = spread([g13])
    act, dact, hid = gate_up(info, t, t_other, w_gate, w_up, (kept0,))

    g13 = by_plane(g13, (hid, g2))
    g13_other = flip(g13, 0)
    g2 = spread([after(g2, g13)])
    sent0 = back(grads0, 0, n, False, (g13,))[0]
    got0 = flip(sent0, 0)
    grads13 = hidden_grads(info, g13, g13_other, 0, act, dact, w_down, (sent0,))
    g2 = joined(info, g2, (grads13[0],))
    g2_other = flip(g2, 0)
    got = flip(back(grads13, 0, 2 * n, False, (g2,))[0], 0)
    kept = back(grads13, 0, 2 * n, True)[0]
    rows13 = [(p * n + c * slots, slots) for c in range(chips) for p in range(2)]
    sum13 = add_split(info, kept, [got], rows13)
    sum0 = add_split(info, kept0, [got0], [(0, n)], (sum13[0],))
    grads2 = hidden_grads(
        info, g2, g2_other, 2 * n, act, dact, w_down, (sum13[0],), True
    )
    got = [flip(x, 0) for x in back(grads2, 0, n, False, (), chips)]
    kept = back(grads2, 0, n, True)[0]
    far1, far3 = fold(sum13, 2)
    sum2 = add_split(info, kept, got, [(0, n)], (far1,))
    piece1, piece3 = plane_shift(far1, EXPERTS - 1), plane_shift(far3, EXPERTS - 3)

    hids, gs = [hid0, hid], [near_g, g13, g2]
    down_grad = down_grads(info, hids, gs, True, None, (sum2[0], far1))
    (far2,) = fold(sum2, 1, (), (down_grad,))
    piece2 = plane_shift(far2, EXPERTS - 2)
    gs = [near_g_other, g13_other, g2_other]
    down_grad = down_grads(info, hids, gs, False, down_grad, (far2, piece1, piece3))
    (piece0,) = fold(sum0, 1, (), (down_grad,))
    pieces = {0: piece0, 1: piece1, 2: piece2, 3: piece3}
    mine, theirs = unpack(
        info,
        expert_ids,
        other_ids,
        [pieces[d] for d in range(EXPERTS)],
        slots,
        capacity,
        (down_grad,),
    )
    got = flip(theirs, 0)
    input_grad = jnp.where(
        core == 0,
        jnp.concatenate([mine, got], axis=1),
        jnp.concatenate([got, mine], axis=1),
    )
    return (input_grad, down_grad[None])


def solution(mesh):
    placed = (
        P(("groups", "expert"), None),
        P(("groups", "expert"), None),
        P(("groups", "expert"), None),
        P("expert", None, None),
        P("expert", None, None),
        P("expert", None, None),
    )
    return jax.shard_map(
        shards,
        mesh=mesh,
        in_specs=placed,
        out_specs=(P(("groups", "expert"), None), P(("groups", "expert"), None, None)),
        check_vma=False,
    )
```
